256 devices in a mesh: sample: 8 (over y, z_hi), slab: 32 (over z_lo, x, core).
Axes of the slice: x: 4, y: 4, z: 8 (z_hi: 2, z_lo: 4; z = z_hi * 4 + z_lo), core: 2. Of those that a mesh axis runs over, the one named last changes fastest.
Arguments:
- volume: bfloat16 [8, 64, 32, 2048], P('sample', 'slab'), may hold values from -6 to 6
- cotangent: bfloat16 [8, 64, 32, 2048], P('sample', 'slab'), may hold values from -6 to 6
- first_weight: bfloat16 [3, 3, 3, 64, 64], replicated, may hold values from -0.15625 to 0.15625
- second_weight: bfloat16 [3, 3, 3, 64, 64], replicated, may hold values from -0.15625 to 0.15625
Outputs:
- features_out: bfloat16 [8, 64, 32, 2048], P('sample', 'slab')
- input_grad: bfloat16 [8, 64, 32, 2048], P('sample', 'slab')
- first_grad: float32 [110592], P(('sample', 'slab'))
- second_grad: float32 [110592], P(('sample', 'slab'))
The draws below stay inside these ranges and needn't reach their ends.
All inputs are finite; a program needn't handle non-finite values.
Results may differ from the reference program's by a relative error of at most 0.024.
Values may be sent and summed in bfloat16 or wider, within the bound.
A program may use at most 64 MiB of HBM per device.

```python
import jax
import jax.numpy as jnp
from jax import lax

C = 64
NY = 32
NZ = 32
SAMPLES = 8
NX = 64
VOXELS = 524288


def steps_of(own_key, shape, split, least, high):
    loudness = 1.0
    for dim, blocks in split:
        draws = jax.random.uniform(jax.random.fold_in(jax.random.fold_in(own_key, 6), dim), (blocks,), jnp.float32, least / len(split), high / len(split))
        loudness = loudness * jnp.repeat(jnp.exp(draws), shape[dim] // blocks).reshape((-1,) + (1,) * (len(shape) - 1 - dim))
    return loudness


def scatter_about(own_key, extent, spread, most, pieces=(), held_as=jnp.bfloat16):
    values = jax.random.normal(own_key, extent, jnp.float32) * spread
    if len(pieces) > 0:
        values = steps_of(own_key, extent, pieces, -0.22, 0.18) * values
    return jnp.clip(values, min=-most, max=most).astype(held_as)


def setup_inputs(seed: int = 0) -> dict:
    arg_keys = jax.random.split(jax.random.key(seed), 5)
    volume = scatter_about(arg_keys[0], (SAMPLES, NX, NY, NZ * C), 1.0, 6.0, ((0, 8), (1, 32)))
    cotangent = scatter_about(arg_keys[1], (SAMPLES, NX, NY, NZ * C), 1.0, 6.0, ((0, 8), (1, 32)))
    first_weight = scatter_about(arg_keys[2], (3, 3, 3, C, C), (27 * C) ** -0.5, 0.15625)
    second_weight = scatter_about(arg_keys[3], (3, 3, 3, C, C), (27 * C) ** -0.5, 0.15625)
    return dict(volume=volume, cotangent=cotangent, first_weight=first_weight, second_weight=second_weight)


def convolve(field, kernel):
    return lax.conv_general_dilated(field, kernel, (1, 1, 1), ((1, 1), (1, 1), (1, 1)), dimension_numbers=('NDHWC', 'DHWIO', 'NDHWC'))

def logistic_gate(preact):
    return preact * jax.nn.sigmoid(preact)

def gate_slope(preact):
    squashed = jax.nn.sigmoid(preact)
    return squashed * (1.0 + preact * (1.0 - squashed))

def reference(volume, cotangent, first_weight, second_weight):
    kernel_one = first_weight.astype(jnp.float32)
    kernel_two = second_weight.astype(jnp.float32)

    def one_sample(sample_pair):
        source, incoming = sample_pair
        field = source.reshape(1, NX, NY, NZ, C).astype(jnp.float32)
        upstream = incoming.reshape(1, NX, NY, NZ, C).astype(jnp.float32)
        first_pre = convolve(field, kernel_one)
        hidden = lax.optimization_barrier(logistic_gate(first_pre).astype(jnp.bfloat16)).astype(jnp.float32)
        second_pre = convolve(hidden, kernel_two)
        result = logistic_gate(second_pre).astype(jnp.bfloat16)
        grad_two = lax.optimization_barrier((upstream * gate_slope(second_pre)).astype(jnp.bfloat16)).astype(jnp.float32)
        unused, pull_two = jax.vjp(convolve, hidden, kernel_two)
        hidden_back, weight_two = pull_two(grad_two)
        grad_one = lax.optimization_barrier((hidden_back * gate_slope(first_pre)).astype(jnp.bfloat16)).astype(jnp.float32)
        unused_one, pull_one = jax.vjp(convolve, field, kernel_one)
        field_back, weight_one = pull_one(grad_one)
        return (result.reshape(NX, NY, NZ * C), field_back.astype(jnp.bfloat16).reshape(NX, NY, NZ * C), weight_one, weight_two)
    results, backs, weights_one, weights_two = lax.map(one_sample, (volume, cotangent))
    norm_factor = 1.0 / jnp.sqrt(jnp.float32(VOXELS))
    first_grad = (lax.optimization_barrier(jnp.sum(weights_one, axis=0)) * norm_factor).reshape(-1)
    second_grad = (lax.optimization_barrier(jnp.sum(weights_two, axis=0)) * norm_factor).reshape(-1)
    return (results, backs, first_grad, second_grad)
```

```python
import functools
import math

import jax
import jax.numpy as jnp
from jax import lax
from jax.experimental import pallas as pl
from jax.experimental.pallas import tpu as pltpu
from jax.sharding import PartitionSpec as P

MESH = pl.DeviceIdType.MESH
BF16 = jnp.bfloat16
F32 = jnp.float32

C = 64
CELLS = 32
MERGED = 2048
QUADS = 8
WINDOW = 384
WIDE = 3 * WINDOW
TAPROWS = 864
OFFSETS = (0, 1, 2, 3, 4, -1)


def dot(a, b):
    return lax.dot_general(a, b, (((1,), (0,)), ((), ())), preferred_element_type=F32)


def sigmoid(v):
    return 0.5 * jnp.tanh(0.5 * v) + 0.5


def prepare(src, plane, win, slot):
    rows = lax.broadcasted_iota(jnp.int32, (CELLS, 128), 0)
    low_half = lax.broadcasted_iota(jnp.int32, (CELLS, 128), 1) < C
    base = slot * 256

    def shifted(tile):
        here = src[plane, :, tile * 128 : tile * 128 + 128].astype(F32)
        before = jnp.where(rows == 0, 0.0, pltpu.roll(here, 1, 0))
        after = jnp.where(rows == CELLS - 1, 0.0, pltpu.roll(here, CELLS - 1, 0))
        return before.astype(BF16), here.astype(BF16), after.astype(BF16)

    nothing = jnp.zeros((CELLS, 128), BF16)
    blank = (nothing, nothing, nothing)
    tiles = {-1: blank, 16: blank}
    for tile in range(16):
        tiles[tile] = shifted(tile)
    for j in range(QUADS):
        at = pl.ds(pl.multiple_of(base + j * CELLS, CELLS), CELLS)
        for d in range(3):
            edge = jnp.where(low_half, tiles[2 * j + 2][d], tiles[2 * j - 1][d])
            win[at, d * WINDOW : d * WINDOW + 128] = tiles[2 * j][d]
            win[at, d * WINDOW + 128 : d * WINDOW + 256] = tiles[2 * j + 1][d]
            win[at, d * WINDOW + 256 : d * WINDOW + 384] = edge


def transpose_plane(win, slot, out, to):
    rows = pl.ds(pl.multiple_of(slot * 256, 256), 256)
    out[pl.ds(pl.multiple_of(to * 256, 256), 256), :] = win[rows, WINDOW : WINDOW + 256].T


def expand_weight(weight, forward, backward):
    zero = jnp.zeros((C, C), BF16)
    blank = jnp.zeros((C, 128), BF16)

    def tap(index, carry):
        kx = index // 3
        ky = index % 3
        m = [weight[kx, ky, kz] for kz in range(3)]
        pair = jnp.concatenate([m[0], m[1]], axis=1).astype(F32).T.astype(BF16)
        last = jnp.concatenate([m[2], zero], axis=1).astype(F32).T.astype(BF16)
        n = [pair[:C], pair[C:], last[:C]]
        cat = lambda a, b: jnp.concatenate([a, b], axis=1)
        ahead = (cat(m[0], zero), cat(m[1], m[0]), cat(m[2], m[1]), cat(zero, m[2]))
        back = (cat(zero, n[0]), cat(n[0], n[1]), cat(n[1], n[2]), cat(n[2], zero))
        for w, offset in enumerate(OFFSETS):
            there = pl.ds(pl.multiple_of(ky * WINDOW + w * C, C), C)
            mirrored = pl.ds(pl.multiple_of((2 - ky) * WINDOW + w * C, C), C)
            for half in range(2):
                a = offset - 2 * half + 1
                b = 2 * half - offset + 2
                cols = slice(128 * half, 128 * half + 128)
                forward[kx, there, cols] = ahead[a] if 0 <= a < 4 else blank
                backward[2 - kx, mirrored, cols] = back[b] if 0 <= b < 4 else blank
        return carry

    lax.fori_loop(0, 9, tap, 0)


def convolve(win, first, planes, weight):
    total = None
    for e in range(3):
        lhs = win[(first + e) * 256 : (first + e + planes) * 256, :]
        term = dot(lhs, weight[e])
        total = term if total is None else total + term
    return total


def kernel_gradient(flipped, win, first, product, flat):
    whole = dot(flipped[0:768], win[first * 256 : first * 256 + 256, :]) + dot(
        flipped[256:1024], win[first * 256 + 256 : first * 256 + 512, :]
    )
    for tile in range(9):
        product[tile] = whole[:, tile * 128 : tile * 128 + 128]
    low_half = lax.broadcasted_iota(jnp.int32, (32, 128), 1) < C

    for e in range(3):
        for ky in range(3):
            column = (2 - ky) * 3

            def part(zi, tile, parity):
                return product[column + tile, pl.ds(e * 256 + zi * C + parity, 32, stride=2), :]

            sums = {}
            for parity in range(2):
                sums[0, parity] = (
                    part(1, 1, parity) + part(3, 2, parity),
                    part(0, 0, parity) + part(2, 1, parity),
                )
                sums[1, parity] = (
                    part(0, 0, parity) + part(2, 1, parity),
                    part(1, 0, parity) + part(3, 1, parity),
                )
                sums[2, parity] = (
                    part(1, 0, parity) + part(3, 1, parity),
                    part(0, 2, parity) + part(2, 0, parity),
                )
            for kz in range(3):
                low0, high0 = sums[kz, 0]
                low1, high1 = sums[kz, 1]
                straight = jnp.where(low_half, low0, high1)
                crossed = jnp.where(low_half, low1, high0)
                tap = (e * 3 + ky) * 3 + kz
                flat[tap * 32 : tap * 32 + 32, :] = straight + pltpu.roll(crossed, C, 1)


def kernel(
    vol_hbm,
    cot_hbm,
    w1_hbm,
    w2_hbm,
    feat_hbm,
    back_hbm,
    first_out,
    second_out,
    vol,
    cot,
    w1,
    w2,
    ahead1,
    back1,
    ahead2,
    back2,
    win_v,
    win_h,
    win_g2,
    win_g1,
    flipped,
    hid,
    g2,
    g1,
    feat,
    back,
    pre,
    own_pre,
    acc,
    product,
    flat,
    near,
    near_in,
    far,
    far_in,
    load_sem,
    store_sem,
    vol_send,
    vol_recv,
    g_send,
    g_recv,
    near_send,
    near_recv,
    far_send,
    far_recv,
    *,
    slabs,
    scale,
):
    sample = lax.axis_index("sample")
    slab = lax.axis_index("slab")
    y, z_hi = sample // 2, sample % 2
    z_lo, x, core = slab // 8, (slab % 8) // 2, slab % 2
    z = z_hi * 4 + z_lo

    def near_partner(r):
        return (((y + r // 4) % 4) * 2 + z_hi, z_lo * 8 + ((x + r % 4) % 4) * 2 + core)

    def far_partner(r):
        zz = (z + r // 2) % 8
        return (y * 2 + zz // 4, (zz % 4) * 8 + x * 2 + (core + r % 2) % 2)

    has_low = slab > 0
    has_high = slab < slabs - 1
    low = (sample, slab - 1)
    high = (sample, slab + 1)

    barrier = pltpu.get_barrier_semaphore()

    @pl.when(has_low)
    def _():
        pl.semaphore_signal(barrier, inc=1, device_id=low, device_id_type=MESH)

    @pl.when(has_high)
    def _():
        pl.semaphore_signal(barrier, inc=1, device_id=high, device_id_type=MESH)

    def greet(r, carry):
        pl.semaphore_signal(barrier, inc=1, device_id=near_partner(r), device_id_type=MESH)
        pl.semaphore_signal(barrier, inc=1, device_id=far_partner(r), device_id_type=MESH)
        return carry

    lax.fori_loop(1, 16, greet, 0)

    loads = [
        pltpu.make_async_copy(w1_hbm, w1, load_sem.at[0]),
        pltpu.make_async_copy(vol_hbm.at[0], vol.at[2:4], load_sem.at[1]),
        pltpu.make_async_copy(w2_hbm, w2, load_sem.at[2]),
        pltpu.make_async_copy(cot_hbm.at[0], cot, load_sem.at[3]),
    ]
    for load in loads:
        load.start()

    neighbours = has_low.astype(jnp.int32) + has_high.astype(jnp.int32)
    pl.semaphore_wait(barrier, 30 + neighbours)

    def to_low(plane):
        return pltpu.make_async_remote_copy(
            vol_hbm.at[0, plane], vol.at[4 + plane], vol_send.at[plane], vol_recv.at[2 + plane], low, MESH
        )

    def to_high(plane):
        return pltpu.make_async_remote_copy(
            vol_hbm.at[0, plane], vol.at[plane], vol_send.at[2 + plane], vol_recv.at[plane], high, MESH
        )

    @pl.when(has_low)
    def _():
        to_low(0).start()

    @pl.when(has_high)
    def _():
        to_high(1).start()

    @pl.when(has_low)
    def _():
        to_low(1).start()

    @pl.when(has_high)
    def _():
        to_high(0).start()

    no_plane = jnp.zeros((CELLS, MERGED), BF16)

    @pl.when(jnp.logical_not(has_low))
    def _():
        for buffer, slots in ((vol, (0, 1)), (g2, (0,)), (g1, (0,))):
            for slot in slots:
                buffer[slot] = no_plane

    @pl.when(jnp.logical_not(has_high))
    def _():
        for buffer, slots in ((vol, (4, 5)), (g2, (3,)), (g1, (3,))):
            for slot in slots:
                buffer[slot] = no_plane

    flat[TAPROWS : TAPROWS + 8, :] = jnp.zeros((8, 128), F32)
    loads[0].wait()
    expand_weight(w1, ahead1, back1)
    loads[1].wait()
    prepare(vol, 2, win_v, 2)
    prepare(vol, 3, win_v, 3)
    loads[2].wait()
    expand_weight(w2, ahead2, back2)

    @pl.when(has_low)
    def _():
        to_high(1).wait_recv()

    @pl.when(has_high)
    def _():
        to_low(0).wait_recv()

    def prepare_pair(src, win, slots):
        def body(i, carry):
            slot = slots[0] + i * (slots[1] - slots[0])
            prepare(src, slot, win, slot)
            return carry

        lax.fori_loop(0, 2, body, 0)

    prepare_pair(vol, win_v, (1, 4))
    own_pre[...] = convolve(win_v, 1, 2, ahead1)

    @pl.when(has_low)
    def _():
        to_high(0).wait_recv()

    @pl.when(has_high)
    def _():
        to_low(1).wait_recv()

    prepare_pair(vol, win_v, (0, 5))
    pre[0:256, :] = convolve(win_v, 0, 1, ahead1)
    pre[256:512, :] = convolve(win_v, 3, 1, ahead1)

    def hide(source, at, plane, keep):
        for j in range(QUADS):
            value = source[pl.ds(pl.multiple_of(at + j * CELLS, CELLS), CELLS), :]
            value = value * sigmoid(value)
            if keep is not None:
                value = jnp.where(keep, value, 0.0)
            hid[plane, :, j * 256 : j * 256 + 256] = value.astype(BF16)

    hide(pre, 0, 0, has_low)
    hide(own_pre, 0, 1, None)
    hide(own_pre, 256, 2, None)
    hide(pre, 256, 3, has_high)
    prepare_pair(hid, win_h, (0, 1))
    prepare_pair(hid, win_h, (2, 3))
    acc[...] = convolve(win_h, 0, 2, ahead2)

    loads[3].wait()

    def second_stage(plane, carry):
        for j in range(QUADS):
            value = acc[pl.ds(pl.multiple_of(plane * 256 + j * CELLS, CELLS), CELLS), :]
            gate = sigmoid(value)
            cols = slice(j * 256, j * 256 + 256)
            feat[plane, :, cols] = (value * gate).astype(BF16)
            slope = gate * (1.0 + value * (1.0 - gate))
            g2[plane + 1, :, cols] = (cot[plane, :, cols].astype(F32) * slope).astype(BF16)
        return carry

    lax.fori_loop(0, 2, second_stage, 0)

    def halo(buffer, which, side):
        if side == 0:
            return pltpu.make_async_remote_copy(
                buffer.at[1], buffer.at[3], g_send.at[2 * which], g_recv.at[2 * which], low, MESH
            )
        return pltpu.make_async_remote_copy(
            buffer.at[2], buffer.at[0], g_send.at[2 * which + 1], g_recv.at[2 * which + 1], high, MESH
        )

    def send_halos(buffer, which):
        @pl.when(has_low)
        def _():
            halo(buffer, which, 0).start()

        @pl.when(has_high)
        def _():
            halo(buffer, which, 1).start()

    def receive_halos(buffer, which):
        @pl.when(has_high)
        def _():
            halo(buffer, which, 0).wait_recv()

        @pl.when(has_low)
        def _():
            halo(buffer, which, 1).wait_recv()

    send_halos(g2, 0)
    features_store = pltpu.make_async_copy(feat, feat_hbm.at[0], store_sem.at[0])
    features_store.start()

    me_near = y * 4 + x

    def near_copy(which, r):
        other = ((y + r // 4) % 4) * 4 + (x + r % 4) % 4
        return pltpu.make_async_remote_copy(
            near.at[which, other],
            near_in.at[which, r],
            near_send.at[which, r],
            near_recv.at[which, r],
            near_partner(r),
            MESH,
        )

    def far_copy(which, r):
        zz = (z + r // 2) % 8
        return pltpu.make_async_remote_copy(
            far.at[which, zz], far_in.at[which, r], far_send.at[which, r], far_recv.at[which, r], far_partner(r), MESH
        )

    def each(copy, what, which):
        def body(r, carry):
            getattr(copy(which, r), what)()
            return carry

        lax.fori_loop(1, 16, body, 0)

    def send_near(which):
        def row(yy, carry):
            for xx in range(4):
                for pair in range(4):
                    starts = [yy * 216 + (2 * pair + i) * 27 + (27 * xx) // 4 for i in range(2)]
                    both = jnp.concatenate([flat[pl.ds(s, 8), :] for s in starts], axis=0)
                    near[which, yy * 4 + xx, 16 * pair : 16 * pair + 16, :] = both.astype(BF16)
            return carry

        lax.fori_loop(0, 4, row, 0)
        each(near_copy, "start", which)

    def send_far(which):
        each(near_copy, "wait_recv", which)
        total = near[which, me_near].astype(F32)
        for r in range(1, 16):
            total = total + near_in[which, r].astype(F32)
        for zz in range(8):
            far[which, zz] = total[8 * zz : 8 * zz + 8]
        each(far_copy, "start", which)

    lane = lax.broadcasted_iota(jnp.int32, (8, 128), 1)
    begin = (96 * x) % 128 + 432 * core
    skip_rows, skip_lanes = begin // 128, begin % 128

    def finish(which, out):
        each(far_copy, "wait_recv", which)
        total = far[which, z]
        for r in range(1, 16):
            total = total + far_in[which, r]
        total = pltpu.roll(total * scale, (128 - skip_lanes) % 128, 1)
        upper = pltpu.roll(total, (8 - skip_rows) % 8, 0)
        lower = pltpu.roll(total, (8 - skip_rows + 7) % 8, 0)
        out[...] = jnp.where(lane < 128 - skip_lanes, upper, lower)

    prepare_pair(g2, win_g2, (1, 2))

    def flip_planes(win, first):
        def body(i, carry):
            transpose_plane(win, first + i, flipped, i)
            return carry

        lax.fori_loop(0, 4, body, 0)

    flip_planes(win_h, 0)
    kernel_gradient(flipped, win_g2, 1, product, flat)
    send_near(1)

    receive_halos(g2, 0)
    prepare_pair(g2, win_g2, (0, 3))
    acc[...] = convolve(win_g2, 0, 2, back2)

    def first_stage(plane, carry):
        for j in range(QUADS):
            at = pl.ds(pl.multiple_of(plane * 256 + j * CELLS, CELLS), CELLS)
            value = own_pre[at, :]
            gate = sigmoid(value)
            slope = gate * (1.0 + value * (1.0 - gate))
            g1[plane + 1, :, j * 256 : j * 256 + 256] = (acc[at, :] * slope).astype(BF16)
        return carry

    lax.fori_loop(0, 2, first_stage, 0)
    send_halos(g1, 1)

    prepare_pair(g1, win_g1, (1, 2))
    flip_planes(win_v, 1)
    kernel_gradient(flipped, win_g1, 1, product, flat)
    send_near(0)
    send_far(1)

    receive_halos(g1, 1)
    prepare_pair(g1, win_g1, (0, 3))
    acc[...] = convolve(win_g1, 0, 2, back1)
    for plane in range(2):
        for j in range(QUADS):
            at = (plane * QUADS + j) * CELLS
            back[plane, :, j * 256 : j * 256 + 256] = acc[at : at + CELLS, :].astype(BF16)
    back_store = pltpu.make_async_copy(back, back_hbm.at[0], store_sem.at[1])
    back_store.start()

    send_far(0)
    finish(1, second_out)
    finish(0, first_out)

    @pl.when(has_low)
    def _():
        to_low(0).wait_send()
        to_low(1).wait_send()
        halo(g2, 0, 0).wait_send()
        halo(g1, 1, 0).wait_send()

    @pl.when(has_high)
    def _():
        to_high(0).wait_send()
        to_high(1).wait_send()
        halo(g2, 0, 1).wait_send()
        halo(g1, 1, 1).wait_send()

    for which in range(2):
        each(near_copy, "wait_send", which)
        each(far_copy, "wait_send", which)
    features_store.wait()
    back_store.wait()


def per_device(volume, cotangent, first_weight, second_weight, *, slabs, voxels):
    vmem = lambda shape, dtype=BF16: pltpu.VMEM(shape, dtype)
    scratch = [
        vmem((6, CELLS, MERGED)),
        vmem((2, CELLS, MERGED)),
        vmem((3, 3, 3, C, C)),
        vmem((3, 3, 3, C, C)),
        vmem((3, WIDE, 256)),
        vmem((3, WIDE, 256)),
        vmem((3, WIDE, 256)),
        vmem((3, WIDE, 256)),
        vmem((6 * 256, WIDE)),
        vmem((4 * 256, WIDE)),
        vmem((4 * 256, WIDE)),
        vmem((4 * 256, WIDE)),
        vmem((1024, 256)),
        vmem((4, CELLS, MERGED)),
        vmem((4, CELLS, MERGED)),
        vmem((4, CELLS, MERGED)),
        vmem((2, CELLS, MERGED)),
        vmem((2, CELLS, MERGED)),
        vmem((512, 256), F32),
        vmem((512, 256), F32),
        vmem((512, 256), F32),
        vmem((9, 768, 128), F32),
        vmem((TAPROWS + 8, 128), F32),
        vmem((2, 16, 64, 128)),
        vmem((2, 16, 64, 128)),
        vmem((2, 8, 8, 128), F32),
        vmem((2, 16, 8, 128), F32),
        pltpu.SemaphoreType.DMA((4,)),
        pltpu.SemaphoreType.DMA((2,)),
        pltpu.SemaphoreType.DMA((4,)),
        pltpu.SemaphoreType.DMA((4,)),
        pltpu.SemaphoreType.DMA((4,)),
        pltpu.SemaphoreType.DMA((4,)),
        pltpu.SemaphoreType.DMA((2, 16)),
        pltpu.SemaphoreType.DMA((2, 16)),
        pltpu.SemaphoreType.DMA((2, 16)),
        pltpu.SemaphoreType.DMA((2, 16)),
    ]
    anywhere = pl.BlockSpec(memory_space=pl.ANY)
    in_vmem = pl.BlockSpec(memory_space=pltpu.VMEM)
    features, back, first, second = pl.pallas_call(
        functools.partial(kernel, slabs=slabs, scale=1.0 / math.sqrt(voxels)),
        out_shape=(
            jax.ShapeDtypeStruct(volume.shape, BF16),
            jax.ShapeDtypeStruct(volume.shape, BF16),
            jax.ShapeDtypeStruct((8, 128), F32),
            jax.ShapeDtypeStruct((8, 128), F32),
        ),
        in_specs=[anywhere] * 4,
        out_specs=(anywhere, anywhere, in_vmem, in_vmem),
        scratch_shapes=scratch,
        compiler_params=pltpu.CompilerParams(
            collective_id=0, has_side_effects=True, vmem_limit_bytes=48 * 2**20
        ),
    )(volume, cotangent, first_weight, second_weight)
    return (features, back, first.reshape(-1)[:432], second.reshape(-1)[:432])


def solution(mesh):
    slabs = mesh.shape["slab"]
    voxels = 524288
    split = P("sample", "slab", None, None)
    return jax.shard_map(
        functools.partial(per_device, slabs=slabs, voxels=voxels),
        mesh=mesh,
        in_specs=(split, split, P(), P()),
        out_specs=(split, split, P(("sample", "slab")), P(("sample", "slab"))),
        check_vma=False,
    )
```

```python
import functools
import math

import jax
import jax.numpy as jnp
from jax import lax
from jax.experimental import pallas as pl
from jax.experimental.pallas import tpu as pltpu
from jax.sharding import PartitionSpec as P

MESH = pl.DeviceIdType.MESH
BF16 = jnp.bfloat16
F32 = jnp.float32

C = 64
CELLS = 32
MERGED = 2048
QUADS = 8
WINDOW = 384
WIDE = 3 * WINDOW
TAPROWS = 864
OFFSETS = (0, 1, 2, 3, 4, -1)


def dot(a, b):
    return lax.dot_general(a, b, (((1,), (0,)), ((), ())), preferred_element_type=F32)


def dot_transposed(a, b):
    return lax.dot_general(a, b, (((1,), (1,)), ((), ())), preferred_element_type=F32)


def sigmoid(v):
    return 0.5 * jnp.tanh(0.5 * v) + 0.5


def prepare(src, plane, win, slot):
    rows = lax.broadcasted_iota(jnp.int32, (CELLS, 128), 0)
    low_half = lax.broadcasted_iota(jnp.int32, (CELLS, 128), 1) < C
    base = slot * 256

    def shifted(tile):
        here = src[plane, :, tile * 128 : tile * 128 + 128].astype(F32)
        before = jnp.where(rows == 0, 0.0, pltpu.roll(here, 1, 0))
        after = jnp.where(rows == CELLS - 1, 0.0, pltpu.roll(here, CELLS - 1, 0))
        return before.astype(BF16), here.astype(BF16), after.astype(BF16)

    nothing = jnp.zeros((CELLS, 128), BF16)
    blank = (nothing, nothing, nothing)
    tiles = {-1: blank, 16: blank}
    for tile in range(16):
        tiles[tile] = shifted(tile)
    for j in range(QUADS):
        at = pl.ds(pl.multiple_of(base + j * CELLS, CELLS), CELLS)
        for d in range(3):
            edge = jnp.where(low_half, tiles[2 * j + 2][d], tiles[2 * j - 1][d])
            win[at, d * WINDOW : d * WINDOW + 128] = tiles[2 * j][d]
            win[at, d * WINDOW + 128 : d * WINDOW + 256] = tiles[2 * j + 1][d]
            win[at, d * WINDOW + 256 : d * WINDOW + 384] = edge


def transpose_plane(win, slot, out, to):
    rows = pl.ds(pl.multiple_of(slot * 256, 256), 256)
    out[pl.ds(pl.multiple_of(to * 256, 256), 256), :] = win[rows, WINDOW : WINDOW + 256].T


def expand_weight(weight, forward, backward):
    zero = jnp.zeros((C, C), BF16)
    blank = jnp.zeros((C, 128), BF16)
    both = lambda a, b: jnp.concatenate([a, b], axis=1)
    for kx in range(3):
        for ky in range(3):
            m = [weight[kx, ky, kz] for kz in range(3)]
            tiles = (both(m[0], zero), both(m[1], m[0]), both(m[2], m[1]), both(zero, m[2]))
            for w, offset in enumerate(OFFSETS):
                there = slice(ky * WINDOW + w * C, ky * WINDOW + w * C + C)
                for half in range(2):
                    a = offset - 2 * half + 1
                    forward[kx, there, 128 * half : 128 * half + 128] = tiles[a] if 0 <= a < 4 else blank
            for zi in range(4):
                for pair in range(3):
                    start = (2 - ky) * WINDOW + 128 * pair
                    a = zi - 2 * pair + 1 if pair < 2 else {0: 3, 3: 0}.get(zi, -1)
                    backward[2 - kx, zi * C : zi * C + C, start : start + 128] = (
                        tiles[a] if 0 <= a < 4 else blank
                    )


def convolve(win, first, planes, weight, mirrored=False):
    product = dot_transposed if mirrored else dot
    total = None
    for e in range(3):
        lhs = win[(first + e) * 256 : (first + e + planes) * 256, :]
        term = product(lhs, weight[e])
        total = term if total is None else total + term
    return total


def kernel_gradient(flipped, win, first, product, flat):
    whole = dot(flipped[0:768], win[first * 256 : first * 256 + 256, :]) + dot(
        flipped[256:1024], win[first * 256 + 256 : first * 256 + 512, :]
    )
    for tile in range(9):
        product[tile] = whole[:, tile * 128 : tile * 128 + 128]
    low_half = lax.broadcasted_iota(jnp.int32, (32, 128), 1) < C

    for e in range(3):
        for ky in range(3):
            column = (2 - ky) * 3

            def part(zi, tile, parity):
                return product[column + tile, pl.ds(e * 256 + zi * C + parity, 32, stride=2), :]

            sums = {}
            for parity in range(2):
                sums[0, parity] = (
                    part(1, 1, parity) + part(3, 2, parity),
                    part(0, 0, parity) + part(2, 1, parity),
                )
                sums[1, parity] = (
                    part(0, 0, parity) + part(2, 1, parity),
                    part(1, 0, parity) + part(3, 1, parity),
                )
                sums[2, parity] = (
                    part(1, 0, parity) + part(3, 1, parity),
                    part(0, 2, parity) + part(2, 0, parity),
                )
            for kz in range(3):
                low0, high0 = sums[kz, 0]
                low1, high1 = sums[kz, 1]
                straight = jnp.where(low_half, low0, high1)
                crossed = jnp.where(low_half, low1, high0)
                tap = (e * 3 + ky) * 3 + kz
                flat[tap * 32 : tap * 32 + 32, :] = straight + pltpu.roll(crossed, C, 1)


def kernel(
    vol_hbm,
    cot_hbm,
    w1_hbm,
    w2_hbm,
    feat_hbm,
    back_hbm,
    first_out,
    second_out,
    vol,
    cot,
    w1,
    w2,
    ahead1,
    back1,
    ahead2,
    back2,
    win_v,
    win_h,
    win_g2,
    win_g1,
    flipped,
    hid,
    g2,
    g1,
    feat,
    back,
    pre,
    own_pre,
    acc,
    product,
    flat,
    near,
    near_in,
    far,
    far_in,
    load_sem,
    store_sem,
    vol_send,
    vol_recv,
    g_send,
    g_recv,
    near_send,
    near_recv,
    far_send,
    far_recv,
    *,
    slabs,
    scale,
):
    sample = lax.axis_index("sample")
    slab = lax.axis_index("slab")
    y, z_hi = sample // 2, sample % 2
    z_lo, x, core = slab // 8, (slab % 8) // 2, slab % 2
    z = z_hi * 4 + z_lo

    def near_partner(r):
        return (lax.rem(y + r // 4, 4) * 2 + z_hi, z_lo * 8 + lax.rem(x + r % 4, 4) * 2 + core)

    def far_partner(r):
        zz = lax.rem(z + r // 2, 8)
        return (y * 2 + lax.div(zz, 4), lax.rem(zz, 4) * 8 + x * 2 + lax.rem(core + r % 2, 2))

    alone = pl.when(slab >= 0)

    has_low = slab > 0
    has_high = slab < slabs - 1
    low = (sample, slab - 1)
    high = (sample, slab + 1)

    barrier = pltpu.get_barrier_semaphore()

    @pl.when(has_low)
    def _():
        pl.semaphore_signal(barrier, inc=1, device_id=low, device_id_type=MESH)

    @pl.when(has_high)
    def _():
        pl.semaphore_signal(barrier, inc=1, device_id=high, device_id_type=MESH)

    for r in range(1, 16):
        pl.semaphore_signal(barrier, inc=1, device_id=near_partner(r), device_id_type=MESH)
        pl.semaphore_signal(barrier, inc=1, device_id=far_partner(r), device_id_type=MESH)

    loads = [
        pltpu.make_async_copy(w1_hbm, w1, load_sem.at[0]),
        pltpu.make_async_copy(vol_hbm.at[0], vol.at[2:4], load_sem.at[1]),
        pltpu.make_async_copy(w2_hbm, w2, load_sem.at[2]),
        pltpu.make_async_copy(cot_hbm.at[0], cot, load_sem.at[3]),
    ]
    for load in loads:
        load.start()

    neighbours = has_low.astype(jnp.int32) + has_high.astype(jnp.int32)
    pl.semaphore_wait(barrier, 30 + neighbours)

    def to_low(plane):
        return pltpu.make_async_remote_copy(
            vol_hbm.at[0, plane], vol.at[4 + plane], vol_send.at[plane], vol_recv.at[2 + plane], low, MESH
        )

    def to_high(plane):
        return pltpu.make_async_remote_copy(
            vol_hbm.at[0, plane], vol.at[plane], vol_send.at[2 + plane], vol_recv.at[plane], high, MESH
        )

    @pl.when(has_low)
    def _():
        to_low(0).start()

    @pl.when(has_high)
    def _():
        to_high(1).start()

    @pl.when(has_low)
    def _():
        to_low(1).start()

    @pl.when(has_high)
    def _():
        to_high(0).start()

    no_plane = jnp.zeros((CELLS, MERGED), BF16)

    @pl.when(jnp.logical_not(has_low))
    def _():
        for buffer, slots in ((vol, (0, 1)), (g2, (0,)), (g1, (0,))):
            for slot in slots:
                buffer[slot] = no_plane

    @pl.when(jnp.logical_not(has_high))
    def _():
        for buffer, slots in ((vol, (4, 5)), (g2, (3,)), (g1, (3,))):
            for slot in slots:
                buffer[slot] = no_plane

    flat[TAPROWS : TAPROWS + 8, :] = jnp.zeros((8, 128), F32)
    loads[0].wait()
    expand_weight(w1, ahead1, back1)
    loads[1].wait()
    prepare(vol, 2, win_v, 2)
    prepare(vol, 3, win_v, 3)
    loads[2].wait()
    expand_weight(w2, ahead2, back2)

    @pl.when(has_low)
    def _():
        to_high(1).wait_recv()

    @pl.when(has_high)
    def _():
        to_low(0).wait_recv()

    def prepare_pair(src, win, slots):
        def body(i, carry):
            slot = slots[0] + i * (slots[1] - slots[0])
            prepare(src, slot, win, slot)
            return carry

        lax.fori_loop(0, 2, body, 0)

    prepare_pair(vol, win_v, (1, 4))
    @alone
    def _():
        own_pre[...] = convolve(win_v, 1, 2, ahead1)


    @pl.when(has_low)
    def _():
        to_high(0).wait_recv()

    @pl.when(has_high)
    def _():
        to_low(1).wait_recv()

    prepare_pair(vol, win_v, (0, 5))
    @alone
    def _():
        pre[0:256, :] = convolve(win_v, 0, 1, ahead1)
        pre[256:512, :] = convolve(win_v, 3, 1, ahead1)


    def hide(source, at, plane, keep):
        for j in range(QUADS):
            value = source[pl.ds(pl.multiple_of(at + j * CELLS, CELLS), CELLS), :]
            value = value * sigmoid(value)
            if keep is not None:
                value = jnp.where(keep, value, 0.0)
            hid[plane, :, j * 256 : j * 256 + 256] = value.astype(BF16)

    hide(pre, 0, 0, has_low)
    hide(own_pre, 0, 1, None)
    hide(own_pre, 256, 2, None)
    hide(pre, 256, 3, has_high)
    prepare_pair(hid, win_h, (0, 1))
    prepare_pair(hid, win_h, (2, 3))
    @alone
    def _():
        acc[...] = convolve(win_h, 0, 2, ahead2)


    loads[3].wait()

    def second_stage(plane, carry):
        for j in range(QUADS):
            value = acc[pl.ds(pl.multiple_of(plane * 256 + j * CELLS, CELLS), CELLS), :]
            gate = sigmoid(value)
            cols = slice(j * 256, j * 256 + 256)
            feat[plane, :, cols] = (value * gate).astype(BF16)
            slope = gate * (1.0 + value * (1.0 - gate))
            g2[plane + 1, :, cols] = (cot[plane, :, cols].astype(F32) * slope).astype(BF16)
        return carry

    lax.fori_loop(0, 2, second_stage, 0)

    def halo(buffer, which, side):
        if side == 0:
            return pltpu.make_async_remote_copy(
                buffer.at[1], buffer.at[3], g_send.at[2 * which], g_recv.at[2 * which], low, MESH
            )
        return pltpu.make_async_remote_copy(
            buffer.at[2], buffer.at[0], g_send.at[2 * which + 1], g_recv.at[2 * which + 1], high, MESH
        )

    def send_halos(buffer, which):
        @pl.when(has_low)
        def _():
            halo(buffer, which, 0).start()

        @pl.when(has_high)
        def _():
            halo(buffer, which, 1).start()

    def receive_halos(buffer, which):
        @pl.when(has_high)
        def _():
            halo(buffer, which, 0).wait_recv()

        @pl.when(has_low)
        def _():
            halo(buffer, which, 1).wait_recv()

    send_halos(g2, 0)
    features_store = pltpu.make_async_copy(feat, feat_hbm.at[0], store_sem.at[0])
    features_store.start()

    me_near = y * 4 + x

    def near_copy(which, r):
        other = lax.rem(y + r // 4, 4) * 4 + lax.rem(x + r % 4, 4)
        return pltpu.make_async_remote_copy(
            near.at[which, other],
            near_in.at[which, r],
            near_send.at[which, r],
            near_recv.at[which, r],
            near_partner(r),
            MESH,
        )

    def far_copy(which, r):
        zz = lax.rem(z + r // 2, 8)
        return pltpu.make_async_remote_copy(
            far.at[which, zz], far_in.at[which, r], far_send.at[which, r], far_recv.at[which, r], far_partner(r), MESH
        )

    def each(copy, what, which):
        for r in range(1, 16):
            getattr(copy(which, r), what)()

    def send_near(which):
        def row(yy, carry):
            for xx in range(4):
                for pair in range(4):
                    starts = [yy * 216 + (2 * pair + i) * 27 + (27 * xx) // 4 for i in range(2)]
                    both = jnp.concatenate([flat[pl.ds(s, 8), :] for s in starts], axis=0)
                    near[which, yy * 4 + xx, 16 * pair : 16 * pair + 16, :] = both.astype(BF16)
            return carry

        lax.fori_loop(0, 4, row, 0)
        each(near_copy, "start", which)

    def send_far(which):
        each(near_copy, "wait_recv", which)
        total = near[which, me_near].astype(F32)
        for r in range(1, 16):
            total = total + near_in[which, r].astype(F32)
        for zz in range(8):
            far[which, zz] = total[8 * zz : 8 * zz + 8]
        each(far_copy, "start", which)

    lane = lax.broadcasted_iota(jnp.int32, (8, 128), 1)
    begin = (96 * x) % 128 + 432 * core
    skip_rows, skip_lanes = begin // 128, begin % 128

    def finish(which, out):
        each(far_copy, "wait_recv", which)
        total = far[which, z]
        for r in range(1, 16):
            total = total + far_in[which, r]
        total = pltpu.roll(total * scale, (128 - skip_lanes) % 128, 1)
        upper = pltpu.roll(total, (8 - skip_rows) % 8, 0)
        lower = pltpu.roll(total, (8 - skip_rows + 7) % 8, 0)
        out[...] = jnp.where(lane < 128 - skip_lanes, upper, lower)

    prepare_pair(g2, win_g2, (1, 2))

    def flip_planes(win, first):
        def body(i, carry):
            transpose_plane(win, first + i, flipped, i)
            return carry

        lax.fori_loop(0, 4, body, 0)

    flip_planes(win_h, 0)
    kernel_gradient(flipped, win_g2, 1, product, flat)
    send_near(1)

    receive_halos(g2, 0)
    prepare_pair(g2, win_g2, (0, 3))
    @alone
    def _():
        acc[...] = convolve(win_g2, 0, 2, back2, True)


    def first_stage(plane, carry):
        for j in range(QUADS):
            at = pl.ds(pl.multiple_of(plane * 256 + j * CELLS, CELLS), CELLS)
            value = own_pre[at, :]
            gate = sigmoid(value)
            slope = gate * (1.0 + value * (1.0 - gate))
            g1[plane + 1, :, j * 256 : j * 256 + 256] = (acc[at, :] * slope).astype(BF16)
        return carry

    lax.fori_loop(0, 2, first_stage, 0)
    send_halos(g1, 1)

    prepare_pair(g1, win_g1, (1, 2))
    flip_planes(win_v, 1)
    kernel_gradient(flipped, win_g1, 1, product, flat)
    send_near(0)
    send_far(1)

    receive_halos(g1, 1)
    prepare_pair(g1, win_g1, (0, 3))
    @alone
    def _():
        acc[...] = convolve(win_g1, 0, 2, back1, True)

    for plane in range(2):
        for j in range(QUADS):
            at = (plane * QUADS + j) * CELLS
            back[plane, :, j * 256 : j * 256 + 256] = acc[at : at + CELLS, :].astype(BF16)
    back_store = pltpu.make_async_copy(back, back_hbm.at[0], store_sem.at[1])
    back_store.start()

    send_far(0)
    finish(1, second_out)
    finish(0, first_out)

    @pl.when(has_low)
    def _():
        to_low(0).wait_send()
        to_low(1).wait_send()
        halo(g2, 0, 0).wait_send()
        halo(g1, 1, 0).wait_send()

    @pl.when(has_high)
    def _():
        to_high(0).wait_send()
        to_high(1).wait_send()
        halo(g2, 0, 1).wait_send()
        halo(g1, 1, 1).wait_send()

    for which in range(2):
        each(near_copy, "wait_send", which)
        each(far_copy, "wait_send", which)
    features_store.wait()
    back_store.wait()


def hand_over(feat_in, back_in, first_in, second_in, feat_out, back_out, first_out, second_out):
    feat_out[...] = feat_in[...]
    back_out[...] = back_in[...]
    for source, target in ((first_in, first_out), (second_in, second_out)):
        for row in range(3):
            target[pl.ds(row * 128, 128)] = source[row]
        target[pl.ds(384, 48)] = source[3, :48]


def per_device(volume, cotangent, first_weight, second_weight, *, slabs, voxels):
    vmem = lambda shape, dtype=BF16: pltpu.VMEM(shape, dtype)
    scratch = [
        vmem((6, CELLS, MERGED)),
        vmem((2, CELLS, MERGED)),
        vmem((3, 3, 3, C, C)),
        vmem((3, 3, 3, C, C)),
        vmem((3, WIDE, 256)),
        vmem((3, 256, WIDE)),
        vmem((3, WIDE, 256)),
        vmem((3, 256, WIDE)),
        vmem((6 * 256, WIDE)),
        vmem((4 * 256, WIDE)),
        vmem((4 * 256, WIDE)),
        vmem((4 * 256, WIDE)),
        vmem((1024, 256)),
        vmem((4, CELLS, MERGED)),
        vmem((4, CELLS, MERGED)),
        vmem((4, CELLS, MERGED)),
        vmem((2, CELLS, MERGED)),
        vmem((2, CELLS, MERGED)),
        vmem((512, 256), F32),
        vmem((512, 256), F32),
        vmem((512, 256), F32),
        vmem((9, 768, 128), F32),
        vmem((TAPROWS + 8, 128), F32),
        vmem((2, 16, 64, 128)),
        vmem((2, 16, 64, 128)),
        vmem((2, 8, 8, 128), F32),
        vmem((2, 16, 8, 128), F32),
        pltpu.SemaphoreType.DMA((4,)),
        pltpu.SemaphoreType.DMA((2,)),
        pltpu.SemaphoreType.DMA((4,)),
        pltpu.SemaphoreType.DMA((4,)),
        pltpu.SemaphoreType.DMA((4,)),
        pltpu.SemaphoreType.DMA((4,)),
        pltpu.SemaphoreType.DMA((2, 16)),
        pltpu.SemaphoreType.DMA((2, 16)),
        pltpu.SemaphoreType.DMA((2, 16)),
        pltpu.SemaphoreType.DMA((2, 16)),
    ]
    anywhere = pl.BlockSpec(memory_space=pl.ANY)
    in_vmem = pl.BlockSpec(memory_space=pltpu.VMEM)
    features, back, first, second = pl.pallas_call(
        functools.partial(kernel, slabs=slabs, scale=1.0 / math.sqrt(voxels)),
        out_shape=(
            jax.ShapeDtypeStruct(volume.shape, BF16),
            jax.ShapeDtypeStruct(volume.shape, BF16),
            jax.ShapeDtypeStruct((8, 128), F32),
            jax.ShapeDtypeStruct((8, 128), F32),
        ),
        in_specs=[anywhere] * 4,
        out_specs=(anywhere, anywhere, in_vmem, in_vmem),
        scratch_shapes=scratch,
        compiler_params=pltpu.CompilerParams(
            collective_id=0, has_side_effects=True, vmem_limit_bytes=63 * 2**20
        ),
    )(volume, cotangent, first_weight, second_weight)
    return pl.pallas_call(
        hand_over,
        out_shape=(
            jax.ShapeDtypeStruct(volume.shape, BF16),
            jax.ShapeDtypeStruct(volume.shape, BF16),
            jax.ShapeDtypeStruct((432,), F32),
            jax.ShapeDtypeStruct((432,), F32),
        ),
        in_specs=[in_vmem] * 4,
        out_specs=(in_vmem,) * 4,
    )(features, back, first, second)


def solution(mesh):
    slabs = mesh.shape["slab"]
    voxels = 524288
    split = P("sample", "slab", None, None)
    return jax.shard_map(
        functools.partial(per_device, slabs=slabs, voxels=voxels),
        mesh=mesh,
        in_specs=(split, split, P(), P()),
        out_specs=(split, split, P(("sample", "slab")), P(("sample", "slab"))),
        check_vma=False,
    )
```

```python
import functools
import math

import jax
import jax.numpy as jnp
from jax import lax
from jax.experimental import pallas as pl
from jax.experimental.pallas import tpu as pltpu
from jax.sharding import PartitionSpec as P

MESH = pl.DeviceIdType.MESH
BF16 = jnp.bfloat16
F32 = jnp.float32

C = 64
CELLS = 32
MERGED = 2048
QUADS = 8
WINDOW = 384
WIDE = 3 * WINDOW
TAPROWS = 864
OFFSETS = (0, 1, 2, 3, 4, -1)


def dot(a, b):
    return lax.dot_general(a, b, (((1,), (0,)), ((), ())), preferred_element_type=F32)


def dot_transposed(a, b):
    return lax.dot_general(a, b, (((1,), (1,)), ((), ())), preferred_element_type=F32)


def sigmoid(v):
    return 0.5 * jnp.tanh(0.5 * v) + 0.5


def prepare(src, plane, win, slot):
    rows = lax.broadcasted_iota(jnp.int32, (CELLS, 128), 0)
    low_half = lax.broadcasted_iota(jnp.int32, (CELLS, 128), 1) < C
    base = slot * 256

    def shifted(tile):
        here = src[plane, :, tile * 128 : tile * 128 + 128].astype(F32)
        before = jnp.where(rows == 0, 0.0, pltpu.roll(here, 1, 0))
        after = jnp.where(rows == CELLS - 1, 0.0, pltpu.roll(here, CELLS - 1, 0))
        return before.astype(BF16), here.astype(BF16), after.astype(BF16)

    nothing = jnp.zeros((CELLS, 128), BF16)
    blank = (nothing, nothing, nothing)
    tiles = {-1: blank, 16: blank}
    for tile in range(16):
        tiles[tile] = shifted(tile)
    for j in range(QUADS):
        at = pl.ds(pl.multiple_of(base + j * CELLS, CELLS), CELLS)
        for d in range(3):
            edge = jnp.where(low_half, tiles[2 * j + 2][d], tiles[2 * j - 1][d])
            win[at, d * WINDOW : d * WINDOW + 128] = tiles[2 * j][d]
            win[at, d * WINDOW + 128 : d * WINDOW + 256] = tiles[2 * j + 1][d]
            win[at, d * WINDOW + 256 : d * WINDOW + 384] = edge


def transpose_plane(win, slot, out, to):
    rows = pl.ds(pl.multiple_of(slot * 256, 256), 256)
    out[pl.ds(pl.multiple_of(to * 256, 256), 256), :] = win[rows, WINDOW : WINDOW + 256].T


def expand_weight(weight, forward, backward):
    zero = jnp.zeros((C, C), BF16)
    blank = jnp.zeros((C, 128), BF16)
    both = lambda a, b: jnp.concatenate([a, b], axis=1)
    for kx in range(3):
        for ky in range(3):
            m = [weight[kx, ky, kz] for kz in range(3)]
            tiles = (both(m[0], zero), both(m[1], m[0]), both(m[2], m[1]), both(zero, m[2]))
            for w, offset in enumerate(OFFSETS):
                there = slice(ky * WINDOW + w * C, ky * WINDOW + w * C + C)
                for half in range(2):
                    a = offset - 2 * half + 1
                    forward[kx, there, 128 * half : 128 * half + 128] = tiles[a] if 0 <= a < 4 else blank
            for zi in range(4):
                for pair in range(3):
                    start = (2 - ky) * WINDOW + 128 * pair
                    a = zi - 2 * pair + 1 if pair < 2 else {0: 3, 3: 0}.get(zi, -1)
                    backward[2 - kx, zi * C : zi * C + C, start : start + 128] = (
                        tiles[a] if 0 <= a < 4 else blank
                    )


def planes_of(win, slot, count=1):
    return win[slot * 256 : (slot + count) * 256, :]


def convolve_own(win, slot, weight, out, product=dot):
    middle = product(planes_of(win, slot, 2), weight[1])
    out[0:256, :] = middle[:256] + product(planes_of(win, slot + 1), weight[2])
    out[256:512, :] = middle[256:] + product(planes_of(win, slot), weight[0])


def convolve_outer(win, slot, weight, out, product=dot):
    out[0:256, :] += product(planes_of(win, slot - 1), weight[0])
    out[256:512, :] += product(planes_of(win, slot + 2), weight[2])


def kernel_gradient(flipped, win, first, product, flat, ready):
    low_half = lax.broadcasted_iota(jnp.int32, (32, 128), 1) < C

    for e in range(3):
        whole = dot(planes_of(flipped, e), planes_of(win, first)) + dot(
            planes_of(flipped, e + 1), planes_of(win, first + 1)
        )
        for tile in range(9):
            product[tile, e * 256 : e * 256 + 256, :] = whole[:, tile * 128 : tile * 128 + 128]
        for ky in range(3):
            column = (2 - ky) * 3

            def part(zi, tile, parity):
                return product[column + tile, pl.ds(e * 256 + zi * C + parity, 32, stride=2), :]

            sums = {}
            for parity in range(2):
                sums[0, parity] = (
                    part(1, 1, parity) + part(3, 2, parity),
                    part(0, 0, parity) + part(2, 1, parity),
                )
                sums[1, parity] = (
                    part(0, 0, parity) + part(2, 1, parity),
                    part(1, 0, parity) + part(3, 1, parity),
                )
                sums[2, parity] = (
                    part(1, 0, parity) + part(3, 1, parity),
                    part(0, 2, parity) + part(2, 0, parity),
                )
            for kz in range(3):
                low0, high0 = sums[kz, 0]
                low1, high1 = sums[kz, 1]
                straight = jnp.where(low_half, low0, high1)
                crossed = jnp.where(low_half, low1, high0)
                tap = (e * 3 + ky) * 3 + kz
                flat[tap * 32 : tap * 32 + 32, :] = straight + pltpu.roll(crossed, C, 1)
        ready(e)


def kernel(
    vol_hbm,
    cot_hbm,
    w1_hbm,
    w2_hbm,
    feat_hbm,
    back_hbm,
    first_out,
    second_out,
    vol,
    cot,
    w1,
    w2,
    ahead1,
    back1,
    ahead2,
    back2,
    win_v,
    win_h,
    win_g2,
    win_g1,
    flipped_v,
    flipped_h,
    hid,
    g2,
    g1,
    feat,
    back,
    pre,
    own_pre,
    acc,
    product,
    flat,
    near,
    near_in,
    far,
    far_in,
    load_sem,
    store_sem,
    vol_send,
    vol_recv,
    g_send,
    g_recv,
    near_send,
    near_recv,
    far_send,
    far_recv,
    *,
    slabs,
    scale,
):
    sample = lax.axis_index("sample")
    slab = lax.axis_index("slab")
    y, z_hi = sample // 2, sample % 2
    z_lo, x, core = slab // 8, (slab % 8) // 2, slab % 2
    z = z_hi * 4 + z_lo

    def near_partner(r):
        return (lax.rem(y + r // 4, 4) * 2 + z_hi, z_lo * 8 + lax.rem(x + r % 4, 4) * 2 + core)

    def far_partner(r):
        zz = lax.rem(z + r // 2, 8)
        return (y * 2 + lax.div(zz, 4), lax.rem(zz, 4) * 8 + x * 2 + lax.rem(core + r % 2, 2))

    alone = pl.when(slab >= 0)

    has_low = slab > 0
    has_high = slab < slabs - 1
    low = (sample, slab - 1)
    high = (sample, slab + 1)

    barrier = pltpu.get_barrier_semaphore()

    @pl.when(has_low)
    def _():
        pl.semaphore_signal(barrier, inc=1, device_id=low, device_id_type=MESH)

    @pl.when(has_high)
    def _():
        pl.semaphore_signal(barrier, inc=1, device_id=high, device_id_type=MESH)

    for r in range(1, 16):
        pl.semaphore_signal(barrier, inc=1, device_id=near_partner(r), device_id_type=MESH)
        pl.semaphore_signal(barrier, inc=1, device_id=far_partner(r), device_id_type=MESH)

    loads = [
        pltpu.make_async_copy(w1_hbm, w1, load_sem.at[0]),
        pltpu.make_async_copy(vol_hbm.at[0], vol.at[2:4], load_sem.at[1]),
        pltpu.make_async_copy(w2_hbm, w2, load_sem.at[2]),
        pltpu.make_async_copy(cot_hbm.at[0], cot, load_sem.at[3]),
    ]
    for load in loads:
        load.start()

    neighbours = has_low.astype(jnp.int32) + has_high.astype(jnp.int32)
    pl.semaphore_wait(barrier, 30 + neighbours)

    def to_low(plane):
        return pltpu.make_async_remote_copy(
            vol_hbm.at[0, plane], vol.at[4 + plane], vol_send.at[plane], vol_recv.at[2 + plane], low, MESH
        )

    def to_high(plane):
        return pltpu.make_async_remote_copy(
            vol_hbm.at[0, plane], vol.at[plane], vol_send.at[2 + plane], vol_recv.at[plane], high, MESH
        )

    @pl.when(has_low)
    def _():
        to_low(0).start()

    @pl.when(has_high)
    def _():
        to_high(1).start()

    @pl.when(has_low)
    def _():
        to_low(1).start()

    @pl.when(has_high)
    def _():
        to_high(0).start()

    no_plane = jnp.zeros((CELLS, MERGED), BF16)

    @pl.when(jnp.logical_not(has_low))
    def _():
        for buffer, slots in ((vol, (0, 1)), (g2, (0,)), (g1, (0,))):
            for slot in slots:
                buffer[slot] = no_plane

    @pl.when(jnp.logical_not(has_high))
    def _():
        for buffer, slots in ((vol, (4, 5)), (g2, (3,)), (g1, (3,))):
            for slot in slots:
                buffer[slot] = no_plane

    flat[TAPROWS : TAPROWS + 8, :] = jnp.zeros((8, 128), F32)
    def prepare_pair(src, win, slots):
        def body(i, carry):
            slot = slots[0] + i * (slots[1] - slots[0])
            prepare(src, slot, win, slot)
            return carry

        lax.fori_loop(0, 2, body, 0)

    def hide(source, at, plane, keep):
        for j in range(QUADS):
            value = source[pl.ds(pl.multiple_of(at + j * CELLS, CELLS), CELLS), :]
            value = value * sigmoid(value)
            if keep is not None:
                value = jnp.where(keep, value, 0.0)
            hid[plane, :, j * 256 : j * 256 + 256] = value.astype(BF16)

    loads[0].wait()
    expand_weight(w1, ahead1, back1)
    loads[1].wait()
    prepare_pair(vol, win_v, (2, 3))

    @alone
    def _():
        convolve_own(win_v, 2, ahead1, own_pre)
        pre[0:256, :] = dot(planes_of(win_v, 2), ahead1[2])
        pre[256:512, :] = dot(planes_of(win_v, 3), ahead1[0])

    loads[2].wait()
    expand_weight(w2, ahead2, back2)

    @pl.when(has_low)
    def _():
        to_high(1).wait_recv()

    @pl.when(has_high)
    def _():
        to_low(0).wait_recv()

    prepare_pair(vol, win_v, (1, 4))

    @alone
    def _():
        convolve_outer(win_v, 2, ahead1, own_pre)
        pre[0:256, :] += dot(planes_of(win_v, 1), ahead1[1])
        pre[256:512, :] += dot(planes_of(win_v, 4), ahead1[1])

    hide(own_pre, 0, 1, None)
    hide(own_pre, 256, 2, None)
    prepare_pair(hid, win_h, (1, 2))

    @alone
    def _():
        convolve_own(win_h, 1, ahead2, acc)

    @pl.when(has_low)
    def _():
        to_high(0).wait_recv()

    @pl.when(has_high)
    def _():
        to_low(1).wait_recv()

    prepare_pair(vol, win_v, (0, 5))

    @alone
    def _():
        pre[0:256, :] += dot(planes_of(win_v, 0), ahead1[0])
        pre[256:512, :] += dot(planes_of(win_v, 5), ahead1[2])

    hide(pre, 0, 0, has_low)
    hide(pre, 256, 3, has_high)
    prepare_pair(hid, win_h, (0, 3))

    @alone
    def _():
        convolve_outer(win_h, 1, ahead2, acc)

    loads[3].wait()

    def halo(buffer, which, side):
        if side == 0:
            return pltpu.make_async_remote_copy(
                buffer.at[1], buffer.at[3], g_send.at[2 * which], g_recv.at[2 * which], low, MESH
            )
        return pltpu.make_async_remote_copy(
            buffer.at[2], buffer.at[0], g_send.at[2 * which + 1], g_recv.at[2 * which + 1], high, MESH
        )

    def send_halo(buffer, which, side):
        @pl.when(has_high if side else has_low)
        def _():
            halo(buffer, which, side).start()

    def second_stage(plane, carry):
        for j in range(QUADS):
            value = acc[pl.ds(pl.multiple_of(plane * 256 + j * CELLS, CELLS), CELLS), :]
            gate = sigmoid(value)
            cols = slice(j * 256, j * 256 + 256)
            feat[plane, :, cols] = (value * gate).astype(BF16)
            slope = gate * (1.0 + value * (1.0 - gate))
            g2[plane + 1, :, cols] = (cot[plane, :, cols].astype(F32) * slope).astype(BF16)
        return carry

    second_stage(0, 0)
    send_halo(g2, 0, 0)
    second_stage(1, 0)
    send_halo(g2, 0, 1)

    def receive_halos(buffer, which):
        @pl.when(has_high)
        def _():
            halo(buffer, which, 0).wait_recv()

        @pl.when(has_low)
        def _():
            halo(buffer, which, 1).wait_recv()

    features_store = pltpu.make_async_copy(feat, feat_hbm.at[0], store_sem.at[0])
    features_store.start()

    me_near = y * 4 + x

    def near_copy(which, r):
        other = lax.rem(y + r // 4, 4) * 4 + lax.rem(x + r % 4, 4)
        return pltpu.make_async_remote_copy(
            near.at[which, other],
            near_in.at[which, r],
            near_send.at[which, r],
            near_recv.at[which, r],
            near_partner(r),
            MESH,
        )

    def far_copy(which, r):
        zz = lax.rem(z + r // 2, 8)
        return pltpu.make_async_remote_copy(
            far.at[which, zz], far_in.at[which, r], far_send.at[which, r], far_recv.at[which, r], far_partner(r), MESH
        )

    def each(copy, what, which):
        for r in range(1, 16):
            getattr(copy(which, r), what)()

    def send_near(which, e):
        for yy in (0,), (1,), (2, 3):
            if yy[0] != e:
                continue
            for to in yy:
                away = lax.rem(to - y + 4, 4)
                for xx in range(4):
                    for pair in range(4):
                        starts = [to * 216 + (2 * pair + i) * 27 + (27 * xx) // 4 for i in range(2)]
                        both = jnp.concatenate([flat[pl.ds(s, 8), :] for s in starts], axis=0)
                        near[which, to * 4 + xx, 16 * pair : 16 * pair + 16, :] = both.astype(BF16)
                for rx in range(4):
                    other = lax.rem(x + rx, 4)
                    copy = pltpu.make_async_remote_copy(
                        near.at[which, to * 4 + other],
                        near_in.at[which, away * 4 + rx],
                        near_send.at[which, away * 4 + rx],
                        near_recv.at[which, away * 4 + rx],
                        (to * 2 + z_hi, z_lo * 8 + other * 2 + core),
                        MESH,
                    )
                    if rx:
                        copy.start()
                    else:
                        pl.when(away != 0)(copy.start)

    def send_far(which):
        each(near_copy, "wait_recv", which)
        total = near[which, me_near].astype(F32)
        for r in range(1, 16):
            total = total + near_in[which, r].astype(F32)
        for zz in range(8):
            far[which, zz] = total[8 * zz : 8 * zz + 8]
        each(far_copy, "start", which)

    lane = lax.broadcasted_iota(jnp.int32, (8, 128), 1)
    begin = (96 * x) % 128 + 432 * core
    skip_rows, skip_lanes = begin // 128, begin % 128

    def finish(which, out):
        each(far_copy, "wait_recv", which)
        total = far[which, z]
        for r in range(1, 16):
            total = total + far_in[which, r]
        total = pltpu.roll(total * scale, (128 - skip_lanes) % 128, 1)
        upper = pltpu.roll(total, (8 - skip_rows) % 8, 0)
        lower = pltpu.roll(total, (8 - skip_rows + 7) % 8, 0)
        out[...] = jnp.where(lane < 128 - skip_lanes, upper, lower)

    prepare_pair(g2, win_g2, (1, 2))

    def flip_planes(win, first, out):
        def body(i, carry):
            transpose_plane(win, first + i, out, i)
            return carry

        lax.fori_loop(0, 4, body, 0)

    flip_planes(win_h, 0, flipped_h)
    kernel_gradient(flipped_h, win_g2, 1, product, flat, functools.partial(send_near, 1))
    flip_planes(win_v, 1, flipped_v)

    @alone
    def _():
        convolve_own(win_g2, 1, back2, acc, dot_transposed)

    receive_halos(g2, 0)
    prepare_pair(g2, win_g2, (0, 3))
    @alone
    def _():
        convolve_outer(win_g2, 1, back2, acc, dot_transposed)


    def first_stage(plane, carry):
        for j in range(QUADS):
            at = pl.ds(pl.multiple_of(plane * 256 + j * CELLS, CELLS), CELLS)
            value = own_pre[at, :]
            gate = sigmoid(value)
            slope = gate * (1.0 + value * (1.0 - gate))
            g1[plane + 1, :, j * 256 : j * 256 + 256] = (acc[at, :] * slope).astype(BF16)
        return carry

    first_stage(0, 0)
    send_halo(g1, 1, 0)
    first_stage(1, 0)
    send_halo(g1, 1, 1)

    prepare_pair(g1, win_g1, (1, 2))
    kernel_gradient(flipped_v, win_g1, 1, product, flat, functools.partial(send_near, 0))

    @alone
    def _():
        convolve_own(win_g1, 1, back1, acc, dot_transposed)

    send_far(1)

    receive_halos(g1, 1)
    prepare_pair(g1, win_g1, (0, 3))
    @alone
    def _():
        convolve_outer(win_g1, 1, back1, acc, dot_transposed)

    for plane in range(2):
        for j in range(QUADS):
            at = (plane * QUADS + j) * CELLS
            back[plane, :, j * 256 : j * 256 + 256] = acc[at : at + CELLS, :].astype(BF16)
    back_store = pltpu.make_async_copy(back, back_hbm.at[0], store_sem.at[1])
    back_store.start()

    send_far(0)
    finish(1, second_out)
    finish(0, first_out)

    @pl.when(has_low)
    def _():
        to_low(0).wait_send()
        to_low(1).wait_send()
        halo(g2, 0, 0).wait_send()
        halo(g1, 1, 0).wait_send()

    @pl.when(has_high)
    def _():
        to_high(0).wait_send()
        to_high(1).wait_send()
        halo(g2, 0, 1).wait_send()
        halo(g1, 1, 1).wait_send()

    for which in range(2):
        each(near_copy, "wait_send", which)
        each(far_copy, "wait_send", which)
    features_store.wait()
    back_store.wait()


def hand_over(feat_in, back_in, first_in, second_in, feat_out, back_out, first_out, second_out):
    feat_out[...] = feat_in[...]
    back_out[...] = back_in[...]
    for source, target in ((first_in, first_out), (second_in, second_out)):
        for row in range(3):
            target[pl.ds(row * 128, 128)] = source[row]
        target[pl.ds(384, 48)] = source[3, :48]


def per_device(volume, cotangent, first_weight, second_weight, *, slabs, voxels):
    vmem = lambda shape, dtype=BF16: pltpu.VMEM(shape, dtype)
    scratch = [
        vmem((6, CELLS, MERGED)),
        vmem((2, CELLS, MERGED)),
        vmem((3, 3, 3, C, C)),
        vmem((3, 3, 3, C, C)),
        vmem((3, WIDE, 256)),
        vmem((3, 256, WIDE)),
        vmem((3, WIDE, 256)),
        vmem((3, 256, WIDE)),
        vmem((6 * 256, WIDE)),
        vmem((4 * 256, WIDE)),
        vmem((4 * 256, WIDE)),
        vmem((4 * 256, WIDE)),
        vmem((1024, 256)),
        vmem((1024, 256)),
        vmem((4, CELLS, MERGED)),
        vmem((4, CELLS, MERGED)),
        vmem((4, CELLS, MERGED)),
        vmem((2, CELLS, MERGED)),
        vmem((2, CELLS, MERGED)),
        vmem((512, 256), F32),
        vmem((512, 256), F32),
        vmem((512, 256), F32),
        vmem((9, 768, 128), F32),
        vmem((TAPROWS + 8, 128), F32),
        vmem((2, 16, 64, 128)),
        vmem((2, 16, 64, 128)),
        vmem((2, 8, 8, 128), F32),
        vmem((2, 16, 8, 128), F32),
        pltpu.SemaphoreType.DMA((4,)),
        pltpu.SemaphoreType.DMA((2,)),
        pltpu.SemaphoreType.DMA((4,)),
        pltpu.SemaphoreType.DMA((4,)),
        pltpu.SemaphoreType.DMA((4,)),
        pltpu.SemaphoreType.DMA((4,)),
        pltpu.SemaphoreType.DMA((2, 16)),
        pltpu.SemaphoreType.DMA((2, 16)),
        pltpu.SemaphoreType.DMA((2, 16)),
        pltpu.SemaphoreType.DMA((2, 16)),
    ]
    anywhere = pl.BlockSpec(memory_space=pl.ANY)
    in_vmem = pl.BlockSpec(memory_space=pltpu.VMEM)
    features, back, first, second = pl.pallas_call(
        functools.partial(kernel, slabs=slabs, scale=1.0 / math.sqrt(voxels)),
        out_shape=(
            jax.ShapeDtypeStruct(volume.shape, BF16),
            jax.ShapeDtypeStruct(volume.shape, BF16),
            jax.ShapeDtypeStruct((8, 128), F32),
            jax.ShapeDtypeStruct((8, 128), F32),
        ),
        in_specs=[anywhere] * 4,
        out_specs=(anywhere, anywhere, in_vmem, in_vmem),
        scratch_shapes=scratch,
        compiler_params=pltpu.CompilerParams(
            collective_id=0, has_side_effects=True, vmem_limit_bytes=63 * 2**20
        ),
    )(volume, cotangent, first_weight, second_weight)
    return pl.pallas_call(
        hand_over,
        out_shape=(
            jax.ShapeDtypeStruct(volume.shape, BF16),
            jax.ShapeDtypeStruct(volume.shape, BF16),
            jax.ShapeDtypeStruct((432,), F32),
            jax.ShapeDtypeStruct((432,), F32),
        ),
        in_specs=[in_vmem] * 4,
        out_specs=(in_vmem,) * 4,
    )(features, back, first, second)


def solution(mesh):
    slabs = mesh.shape["slab"]
    voxels = 524288
    split = P("sample", "slab", None, None)
    return jax.shard_map(
        functools.partial(per_device, slabs=slabs, voxels=voxels),
        mesh=mesh,
        in_specs=(split, split, P(), P()),
        out_specs=(split, split, P(("sample", "slab")), P(("sample", "slab"))),
        check_vma=False,
    )
```

```python
import functools
import math

import jax
import jax.numpy as jnp
from jax import lax
from jax.experimental import pallas as pl
from jax.experimental.pallas import tpu as pltpu
from jax.sharding import PartitionSpec as P

MESH = pl.DeviceIdType.MESH
BF16 = jnp.bfloat16
F32 = jnp.float32

C = 64
CELLS = 32
MERGED = 2048
QUADS = 8
WINDOW = 384
WIDE = 3 * WINDOW
TAPROWS = 864
OFFSETS = (0, 1, 2, 3, 4, -1)


def dot(a, b):
    return lax.dot_general(a, b, (((1,), (0,)), ((), ())), preferred_element_type=F32)


def dot_transposed(a, b):
    return lax.dot_general(a, b, (((1,), (1,)), ((), ())), preferred_element_type=F32)


def sigmoid(v):
    return 0.5 * jnp.tanh(0.5 * v) + 0.5


def prepare(src, plane, win, slot):
    rows = lax.broadcasted_iota(jnp.int32, (CELLS, 128), 0)
    low_half = lax.broadcasted_iota(jnp.int32, (CELLS, 128), 1) < C
    base = slot * 256

    def shifted(tile):
        here = src[plane, :, tile * 128 : tile * 128 + 128].astype(F32)
        before = jnp.where(rows == 0, 0.0, pltpu.roll(here, 1, 0))
        after = jnp.where(rows == CELLS - 1, 0.0, pltpu.roll(here, CELLS - 1, 0))
        return before.astype(BF16), here.astype(BF16), after.astype(BF16)

    nothing = jnp.zeros((CELLS, 128), BF16)
    blank = (nothing, nothing, nothing)
    tiles = {-1: blank, 16: blank}
    for tile in range(16):
        tiles[tile] = shifted(tile)
    for j in range(QUADS):
        at = pl.ds(pl.multiple_of(base + j * CELLS, CELLS), CELLS)
        for d in range(3):
            edge = jnp.where(low_half, tiles[2 * j + 2][d], tiles[2 * j - 1][d])
            win[at, d * WINDOW : d * WINDOW + 128] = tiles[2 * j][d]
            win[at, d * WINDOW + 128 : d * WINDOW + 256] = tiles[2 * j + 1][d]
            win[at, d * WINDOW + 256 : d * WINDOW + 384] = edge


def transpose_plane(win, slot, out, to):
    rows = pl.ds(pl.multiple_of(slot * 256, 256), 256)
    out[pl.ds(pl.multiple_of(to * 256, 256), 256), :] = win[rows, WINDOW : WINDOW + 256].T


def expand_weight(weight, forward, backward):
    zero = jnp.zeros((C, C), BF16)
    blank = jnp.zeros((C, 128), BF16)
    both = lambda a, b: jnp.concatenate([a, b], axis=1)
    for kx in range(3):
        for ky in range(3):
            m = [weight[kx, ky, kz] for kz in range(3)]
            tiles = (both(m[0], zero), both(m[1], m[0]), both(m[2], m[1]), both(zero, m[2]))
            for w, offset in enumerate(OFFSETS):
                there = slice(ky * WINDOW + w * C, ky * WINDOW + w * C + C)
                for half in range(2):
                    a = offset - 2 * half + 1
                    forward[kx, there, 128 * half : 128 * half + 128] = tiles[a] if 0 <= a < 4 else blank
            for zi in range(4):
                for pair in range(3):
                    start = (2 - ky) * WINDOW + 128 * pair
                    a = zi - 2 * pair + 1 if pair < 2 else {0: 3, 3: 0}.get(zi, -1)
                    backward[2 - kx, zi * C : zi * C + C, start : start + 128] = (
                        tiles[a] if 0 <= a < 4 else blank
                    )


def planes_of(win, slot, count=1):
    if isinstance(slot, int):
        return win[slot * 256 : (slot + count) * 256, :]
    return win[pl.ds(pl.multiple_of(slot * 256, 256), count * 256), :]


def convolve_own(win, slot, weight, out, product=dot):
    middle = product(planes_of(win, slot, 2), weight[1])
    out[0:256, :] = middle[:256] + product(planes_of(win, slot + 1), weight[2])
    out[256:512, :] = middle[256:] + product(planes_of(win, slot), weight[0])


def add_outer(win, slot, weight, out, side, product=dot):
    at = pl.ds(pl.multiple_of(side * 256, 256), 256)
    out[at, :] += product(planes_of(win, slot), weight[2 * side])


def kernel_gradient(flipped, win, first, product, flat, ready):
    low_half = lax.broadcasted_iota(jnp.int32, (32, 128), 1) < C

    for e in range(3):
        whole = dot(planes_of(flipped, e), planes_of(win, first)) + dot(
            planes_of(flipped, e + 1), planes_of(win, first + 1)
        )
        for tile in range(9):
            product[tile, e * 256 : e * 256 + 256, :] = whole[:, tile * 128 : tile * 128 + 128]
        for ky in range(3):
            column = (2 - ky) * 3

            def part(zi, tile, parity):
                return product[column + tile, pl.ds(e * 256 + zi * C + parity, 32, stride=2), :]

            sums = {}
            for parity in range(2):
                sums[0, parity] = (
                    part(1, 1, parity) + part(3, 2, parity),
                    part(0, 0, parity) + part(2, 1, parity),
                )
                sums[1, parity] = (
                    part(0, 0, parity) + part(2, 1, parity),
                    part(1, 0, parity) + part(3, 1, parity),
                )
                sums[2, parity] = (
                    part(1, 0, parity) + part(3, 1, parity),
                    part(0, 2, parity) + part(2, 0, parity),
                )
            for kz in range(3):
                low0, high0 = sums[kz, 0]
                low1, high1 = sums[kz, 1]
                straight = jnp.where(low_half, low0, high1)
                crossed = jnp.where(low_half, low1, high0)
                tap = (e * 3 + ky) * 3 + kz
                flat[tap * 32 : tap * 32 + 32, :] = straight + pltpu.roll(crossed, C, 1)
        ready(e)


def kernel(
    vol_hbm,
    cot_hbm,
    w1_hbm,
    w2_hbm,
    feat_hbm,
    back_hbm,
    first_out,
    second_out,
    vol,
    cot,
    w1,
    w2,
    ahead1,
    back1,
    ahead2,
    back2,
    win_v,
    win_h,
    win_g2,
    win_g1,
    flipped_v,
    flipped_h,
    hid,
    g2,
    g1,
    feat,
    back,
    pre,
    own_pre,
    acc,
    product,
    flat,
    near,
    near_in,
    far,
    far_in,
    load_sem,
    store_sem,
    vol_send,
    vol_recv,
    g_send,
    g_recv,
    near_send,
    near_recv,
    far_send,
    far_recv,
    *,
    slabs,
    scale,
):
    sample = lax.axis_index("sample")
    slab = lax.axis_index("slab")
    y, z_hi = sample // 2, sample % 2
    z_lo, x, core = slab // 8, (slab % 8) // 2, slab % 2
    z = z_hi * 4 + z_lo

    def near_partner(r):
        return (lax.rem(y + r // 4, 4) * 2 + z_hi, z_lo * 8 + lax.rem(x + r % 4, 4) * 2 + core)

    def far_partner(r):
        zz = lax.rem(z + r // 2, 8)
        return (y * 2 + lax.div(zz, 4), lax.rem(zz, 4) * 8 + x * 2 + lax.rem(core + r % 2, 2))

    alone = pl.when(slab >= 0)

    has_low = slab > 0
    has_high = slab < slabs - 1
    low = (sample, slab - 1)
    high = (sample, slab + 1)

    barrier = pltpu.get_barrier_semaphore()

    @pl.when(has_low)
    def _():
        pl.semaphore_signal(barrier, inc=1, device_id=low, device_id_type=MESH)

    @pl.when(has_high)
    def _():
        pl.semaphore_signal(barrier, inc=1, device_id=high, device_id_type=MESH)

    for r in range(1, 16):
        pl.semaphore_signal(barrier, inc=1, device_id=near_partner(r), device_id_type=MESH)
        pl.semaphore_signal(barrier, inc=1, device_id=far_partner(r), device_id_type=MESH)

    loads = [
        pltpu.make_async_copy(w1_hbm, w1, load_sem.at[0]),
        pltpu.make_async_copy(vol_hbm.at[0], vol.at[2:4], load_sem.at[1]),
        pltpu.make_async_copy(w2_hbm, w2, load_sem.at[2]),
        pltpu.make_async_copy(cot_hbm.at[0], cot, load_sem.at[3]),
    ]
    for load in loads:
        load.start()

    neighbours = has_low.astype(jnp.int32) + has_high.astype(jnp.int32)
    pl.semaphore_wait(barrier, 30 + neighbours)

    def to_low(plane):
        return pltpu.make_async_remote_copy(
            vol_hbm.at[0, plane], vol.at[4 + plane], vol_send.at[plane], vol_recv.at[2 + plane], low, MESH
        )

    def to_high(plane):
        return pltpu.make_async_remote_copy(
            vol_hbm.at[0, plane], vol.at[plane], vol_send.at[2 + plane], vol_recv.at[plane], high, MESH
        )

    @pl.when(has_low)
    def _():
        to_low(0).start()

    @pl.when(has_high)
    def _():
        to_high(1).start()

    @pl.when(has_low)
    def _():
        to_low(1).start()

    @pl.when(has_high)
    def _():
        to_high(0).start()

    no_plane = jnp.zeros((CELLS, MERGED), BF16)

    @pl.when(jnp.logical_not(has_low))
    def _():
        for buffer, slots in ((vol, (0, 1)), (g2, (0,)), (g1, (0,))):
            for slot in slots:
                buffer[slot] = no_plane

    @pl.when(jnp.logical_not(has_high))
    def _():
        for buffer, slots in ((vol, (4, 5)), (g2, (3,)), (g1, (3,))):
            for slot in slots:
                buffer[slot] = no_plane

    flat[TAPROWS : TAPROWS + 8, :] = jnp.zeros((8, 128), F32)
    def prepare_pair(src, win, slots):
        def body(i, carry):
            slot = slots[0] + i * (slots[1] - slots[0])
            prepare(src, slot, win, slot)
            return carry

        lax.fori_loop(0, 2, body, 0)

    def hide(source, at, plane, keep):
        for j in range(QUADS):
            value = source[pl.ds(pl.multiple_of(at + j * CELLS, CELLS), CELLS), :]
            value = value * sigmoid(value)
            if keep is not None:
                value = jnp.where(keep, value, 0.0)
            hid[plane, :, j * 256 : j * 256 + 256] = value.astype(BF16)

    loads[0].wait()
    expand_weight(w1, ahead1, back1)
    loads[1].wait()
    prepare_pair(vol, win_v, (2, 3))

    @alone
    def _():
        convolve_own(win_v, 2, ahead1, own_pre)
        pre[0:256, :] = dot(planes_of(win_v, 2), ahead1[2])
        pre[256:512, :] = dot(planes_of(win_v, 3), ahead1[0])

    loads[2].wait()
    expand_weight(w2, ahead2, back2)

    def on_side(side, act_low, act_high):
        pl.when(jnp.logical_and(side == 0, has_low))(act_low)
        pl.when(jnp.logical_and(side == 1, has_high))(act_high)

    def side_of(i):
        return lax.rem(1 - core + i, 2)

    def volume_side(i, carry):
        side = side_of(i)
        on_side(side, lambda: to_high(1).wait_recv(), lambda: to_low(0).wait_recv())
        slot = 1 + 3 * side
        prepare(vol, slot, win_v, slot)

        @alone
        def _():
            add_outer(win_v, slot, ahead1, own_pre, side)
            at = pl.ds(pl.multiple_of(side * 256, 256), 256)
            pre[at, :] += dot(planes_of(win_v, slot), ahead1[1])

        hide(own_pre, side * 256, 1 + side, None)
        prepare(hid, 1 + side, win_h, 1 + side)

        @pl.when(i == 1)
        def _():
            convolve_own(win_h, 1, ahead2, acc)
            add_outer(win_h, 3 * (1 - side), ahead2, acc, 1 - side)

        on_side(side, lambda: to_high(0).wait_recv(), lambda: to_low(1).wait_recv())
        prepare(vol, 5 * side, win_v, 5 * side)

        @alone
        def _():
            add_outer(win_v, 5 * side, ahead1, pre, side)

        inside = jnp.logical_or(jnp.logical_and(side == 0, has_low), jnp.logical_and(side == 1, has_high))
        hide(pre, side * 256, 3 * side, inside)
        prepare(hid, 3 * side, win_h, 3 * side)
        return carry

    lax.fori_loop(0, 2, volume_side, 0)

    @alone
    def _():
        side = side_of(1)
        add_outer(win_h, 3 * side, ahead2, acc, side)

    loads[3].wait()

    def halo(buffer, which, side):
        if side == 0:
            return pltpu.make_async_remote_copy(
                buffer.at[1], buffer.at[3], g_send.at[2 * which], g_recv.at[2 * which], low, MESH
            )
        return pltpu.make_async_remote_copy(
            buffer.at[2], buffer.at[0], g_send.at[2 * which + 1], g_recv.at[2 * which + 1], high, MESH
        )

    def send_halo(buffer, which, side):
        @pl.when(has_high if side else has_low)
        def _():
            halo(buffer, which, side).start()

    def second_stage(plane, carry):
        for j in range(QUADS):
            value = acc[pl.ds(pl.multiple_of(plane * 256 + j * CELLS, CELLS), CELLS), :]
            gate = sigmoid(value)
            cols = slice(j * 256, j * 256 + 256)
            feat[plane, :, cols] = (value * gate).astype(BF16)
            slope = gate * (1.0 + value * (1.0 - gate))
            g2[plane + 1, :, cols] = (cot[plane, :, cols].astype(F32) * slope).astype(BF16)
        return carry

    second_stage(0, 0)
    send_halo(g2, 0, 0)
    second_stage(1, 0)
    send_halo(g2, 0, 1)

    features_store = pltpu.make_async_copy(feat, feat_hbm.at[0], store_sem.at[0])
    features_store.start()

    me_near = y * 4 + x

    def near_copy(which, r):
        other = lax.rem(y + r // 4, 4) * 4 + lax.rem(x + r % 4, 4)
        return pltpu.make_async_remote_copy(
            near.at[which, other],
            near_in.at[which, r],
            near_send.at[which, r],
            near_recv.at[which, r],
            near_partner(r),
            MESH,
        )

    def far_copy(which, r):
        zz = lax.rem(z + r // 2, 8)
        return pltpu.make_async_remote_copy(
            far.at[which, zz], far_in.at[which, r], far_send.at[which, r], far_recv.at[which, r], far_partner(r), MESH
        )

    def each(copy, what, which):
        for r in range(1, 16):
            getattr(copy(which, r), what)()

    def send_near(which, e):
        for yy in (0,), (1,), (2, 3):
            if yy[0] != e:
                continue
            for to in yy:
                away = lax.rem(to - y + 4, 4)
                for xx in range(4):
                    for pair in range(4):
                        starts = [to * 216 + (2 * pair + i) * 27 + (27 * xx) // 4 for i in range(2)]
                        both = jnp.concatenate([flat[pl.ds(s, 8), :] for s in starts], axis=0)
                        near[which, to * 4 + xx, 16 * pair : 16 * pair + 16, :] = both.astype(BF16)
                for rx in range(4):
                    other = lax.rem(x + rx, 4)
                    copy = pltpu.make_async_remote_copy(
                        near.at[which, to * 4 + other],
                        near_in.at[which, away * 4 + rx],
                        near_send.at[which, away * 4 + rx],
                        near_recv.at[which, away * 4 + rx],
                        (to * 2 + z_hi, z_lo * 8 + other * 2 + core),
                        MESH,
                    )
                    if rx:
                        copy.start()
                    else:
                        pl.when(away != 0)(copy.start)

    def send_far(which):
        each(near_copy, "wait_recv", which)
        total = near[which, me_near].astype(F32)
        for r in range(1, 16):
            total = total + near_in[which, r].astype(F32)
        for zz in range(8):
            far[which, zz] = total[8 * zz : 8 * zz + 8]
        each(far_copy, "start", which)

    lane = lax.broadcasted_iota(jnp.int32, (8, 128), 1)
    begin = (96 * x) % 128 + 432 * core
    skip_rows, skip_lanes = begin // 128, begin % 128

    def finish(which, out):
        each(far_copy, "wait_recv", which)
        total = far[which, z]
        for r in range(1, 16):
            total = total + far_in[which, r]
        total = pltpu.roll(total * scale, (128 - skip_lanes) % 128, 1)
        upper = pltpu.roll(total, (8 - skip_rows) % 8, 0)
        lower = pltpu.roll(total, (8 - skip_rows + 7) % 8, 0)
        out[...] = jnp.where(lane < 128 - skip_lanes, upper, lower)

    prepare_pair(g2, win_g2, (1, 2))

    def flip_planes(win, first, out):
        def body(i, carry):
            transpose_plane(win, first + i, out, i)
            return carry

        lax.fori_loop(0, 4, body, 0)

    flip_planes(win_h, 0, flipped_h)
    kernel_gradient(flipped_h, win_g2, 1, product, flat, functools.partial(send_near, 1))
    flip_planes(win_v, 1, flipped_v)

    @alone
    def _():
        convolve_own(win_g2, 1, back2, acc, dot_transposed)

    def first_stage(plane, carry):
        for j in range(QUADS):
            at = pl.ds(pl.multiple_of(plane * 256 + j * CELLS, CELLS), CELLS)
            value = own_pre[at, :]
            gate = sigmoid(value)
            slope = gate * (1.0 + value * (1.0 - gate))
            g1[plane + 1, :, j * 256 : j * 256 + 256] = (acc[at, :] * slope).astype(BF16)
        return carry

    def receive_side(buffer, which, side):
        on_side(
            side,
            lambda: halo(buffer, which, 1).wait_recv(),
            lambda: halo(buffer, which, 0).wait_recv(),
        )

    def g2_side(i, carry):
        side = side_of(i)
        receive_side(g2, 0, side)
        prepare(g2, 3 * side, win_g2, 3 * side)

        @alone
        def _():
            add_outer(win_g2, 3 * side, back2, acc, side, dot_transposed)

        first_stage(side, 0)
        on_side(side, lambda: halo(g1, 1, 0).start(), lambda: halo(g1, 1, 1).start())
        prepare(g1, 1 + side, win_g1, 1 + side)
        return carry

    lax.fori_loop(0, 2, g2_side, 0)
    kernel_gradient(flipped_v, win_g1, 1, product, flat, functools.partial(send_near, 0))

    @alone
    def _():
        convolve_own(win_g1, 1, back1, acc, dot_transposed)

    send_far(1)

    def g1_side(i, carry):
        side = side_of(i)
        receive_side(g1, 1, side)
        prepare(g1, 3 * side, win_g1, 3 * side)

        @alone
        def _():
            add_outer(win_g1, 3 * side, back1, acc, side, dot_transposed)

        return carry

    lax.fori_loop(0, 2, g1_side, 0)
    for plane in range(2):
        for j in range(QUADS):
            at = (plane * QUADS + j) * CELLS
            back[plane, :, j * 256 : j * 256 + 256] = acc[at : at + CELLS, :].astype(BF16)
    back_store = pltpu.make_async_copy(back, back_hbm.at[0], store_sem.at[1])
    back_store.start()

    send_far(0)
    finish(1, second_out)
    finish(0, first_out)

    @pl.when(has_low)
    def _():
        to_low(0).wait_send()
        to_low(1).wait_send()
        halo(g2, 0, 0).wait_send()
        halo(g1, 1, 0).wait_send()

    @pl.when(has_high)
    def _():
        to_high(0).wait_send()
        to_high(1).wait_send()
        halo(g2, 0, 1).wait_send()
        halo(g1, 1, 1).wait_send()

    for which in range(2):
        each(near_copy, "wait_send", which)
        each(far_copy, "wait_send", which)
    features_store.wait()
    back_store.wait()


def hand_over(feat_in, back_in, first_in, second_in, feat_out, back_out, first_out, second_out):
    feat_out[...] = feat_in[...]
    back_out[...] = back_in[...]
    for source, target in ((first_in, first_out), (second_in, second_out)):
        for row in range(3):
            target[pl.ds(row * 128, 128)] = source[row]
        target[pl.ds(384, 48)] = source[3, :48]


def per_device(volume, cotangent, first_weight, second_weight, *, slabs, voxels):
    vmem = lambda shape, dtype=BF16: pltpu.VMEM(shape, dtype)
    scratch = [
        vmem((6, CELLS, MERGED)),
        vmem((2, CELLS, MERGED)),
        vmem((3, 3, 3, C, C)),
        vmem((3, 3, 3, C, C)),
        vmem((3, WIDE, 256)),
        vmem((3, 256, WIDE)),
        vmem((3, WIDE, 256)),
        vmem((3, 256, WIDE)),
        vmem((6 * 256, WIDE)),
        vmem((4 * 256, WIDE)),
        vmem((4 * 256, WIDE)),
        vmem((4 * 256, WIDE)),
        vmem((1024, 256)),
        vmem((1024, 256)),
        vmem((4, CELLS, MERGED)),
        vmem((4, CELLS, MERGED)),
        vmem((4, CELLS, MERGED)),
        vmem((2, CELLS, MERGED)),
        vmem((2, CELLS, MERGED)),
        vmem((512, 256), F32),
        vmem((512, 256), F32),
        vmem((512, 256), F32),
        vmem((9, 768, 128), F32),
        vmem((TAPROWS + 8, 128), F32),
        vmem((2, 16, 64, 128)),
        vmem((2, 16, 64, 128)),
        vmem((2, 8, 8, 128), F32),
        vmem((2, 16, 8, 128), F32),
        pltpu.SemaphoreType.DMA((4,)),
        pltpu.SemaphoreType.DMA((2,)),
        pltpu.SemaphoreType.DMA((4,)),
        pltpu.SemaphoreType.DMA((4,)),
        pltpu.SemaphoreType.DMA((4,)),
        pltpu.SemaphoreType.DMA((4,)),
        pltpu.SemaphoreType.DMA((2, 16)),
        pltpu.SemaphoreType.DMA((2, 16)),
        pltpu.SemaphoreType.DMA((2, 16)),
        pltpu.SemaphoreType.DMA((2, 16)),
    ]
    anywhere = pl.BlockSpec(memory_space=pl.ANY)
    in_vmem = pl.BlockSpec(memory_space=pltpu.VMEM)
    features, back, first, second = pl.pallas_call(
        functools.partial(kernel, slabs=slabs, scale=1.0 / math.sqrt(voxels)),
        out_shape=(
            jax.ShapeDtypeStruct(volume.shape, BF16),
            jax.ShapeDtypeStruct(volume.shape, BF16),
            jax.ShapeDtypeStruct((8, 128), F32),
            jax.ShapeDtypeStruct((8, 128), F32),
        ),
        in_specs=[anywhere] * 4,
        out_specs=(anywhere, anywhere, in_vmem, in_vmem),
        scratch_shapes=scratch,
        compiler_params=pltpu.CompilerParams(
            collective_id=0, has_side_effects=True, vmem_limit_bytes=63 * 2**20
        ),
    )(volume, cotangent, first_weight, second_weight)
    return pl.pallas_call(
        hand_over,
        out_shape=(
            jax.ShapeDtypeStruct(volume.shape, BF16),
            jax.ShapeDtypeStruct(volume.shape, BF16),
            jax.ShapeDtypeStruct((432,), F32),
            jax.ShapeDtypeStruct((432,), F32),
        ),
        in_specs=[in_vmem] * 4,
        out_specs=(in_vmem,) * 4,
    )(features, back, first, second)


def solution(mesh):
    slabs = mesh.shape["slab"]
    voxels = 524288
    split = P("sample", "slab", None, None)
    return jax.shard_map(
        functools.partial(per_device, slabs=slabs, voxels=voxels),
        mesh=mesh,
        in_specs=(split, split, P(), P()),
        out_specs=(split, split, P(("sample", "slab")), P(("sample", "slab"))),
        check_vma=False,
    )
```

```python
import functools
import math

import jax
import jax.numpy as jnp
from jax import lax
from jax.experimental import pallas as pl
from jax.experimental.pallas import tpu as pltpu
from jax.sharding import PartitionSpec as P

MESH = pl.DeviceIdType.MESH
BF16 = jnp.bfloat16
F32 = jnp.float32

C = 64
CELLS = 32
MERGED = 2048
QUADS = 8
WINDOW = 384
WIDE = 3 * WINDOW
TAPROWS = 864
OFFSETS = (0, 1, 2, 3, 4, -1)


def dot(a, b):
    return lax.dot_general(a, b, (((1,), (0,)), ((), ())), preferred_element_type=F32)


def dot_transposed(a, b):
    return lax.dot_general(a, b, (((1,), (1,)), ((), ())), preferred_element_type=F32)


def sigmoid(v):
    return 0.5 * jnp.tanh(0.5 * v) + 0.5


def prepare(src, plane, win, slot):
    rows = lax.broadcasted_iota(jnp.int32, (CELLS, 128), 0)
    low_half = lax.broadcasted_iota(jnp.int32, (CELLS, 128), 1) < C
    base = slot * 256

    def shifted(tile):
        here = src[plane, :, tile * 128 : tile * 128 + 128].astype(F32)
        before = jnp.where(rows == 0, 0.0, pltpu.roll(here, 1, 0))
        after = jnp.where(rows == CELLS - 1, 0.0, pltpu.roll(here, CELLS - 1, 0))
        return before.astype(BF16), here.astype(BF16), after.astype(BF16)

    nothing = jnp.zeros((CELLS, 128), BF16)
    blank = (nothing, nothing, nothing)
    tiles = {-1: blank, 16: blank}
    for tile in range(16):
        tiles[tile] = shifted(tile)
    for j in range(QUADS):
        at = pl.ds(pl.multiple_of(base + j * CELLS, CELLS), CELLS)
        for d in range(3):
            edge = jnp.where(low_half, tiles[2 * j + 2][d], tiles[2 * j - 1][d])
            win[at, d * WINDOW : d * WINDOW + 128] = tiles[2 * j][d]
            win[at, d * WINDOW + 128 : d * WINDOW + 256] = tiles[2 * j + 1][d]
            win[at, d * WINDOW + 256 : d * WINDOW + 384] = edge


def transpose_plane(win, slot, out, to):
    rows = pl.ds(pl.multiple_of(slot * 256, 256), 256)
    out[pl.ds(pl.multiple_of(to * 256, 256), 256), :] = win[rows, WINDOW : WINDOW + 256].T


def expand_weight(weight, forward, backward):
    zero = jnp.zeros((C, C), BF16)
    blank = jnp.zeros((C, 128), BF16)
    both = lambda a, b: jnp.concatenate([a, b], axis=1)
    for kx in range(3):
        for ky in range(3):
            m = [weight[kx, ky, kz] for kz in range(3)]
            tiles = (both(m[0], zero), both(m[1], m[0]), both(m[2], m[1]), both(zero, m[2]))
            for w, offset in enumerate(OFFSETS):
                there = slice(ky * WINDOW + w * C, ky * WINDOW + w * C + C)
                for half in range(2):
                    a = offset - 2 * half + 1
                    forward[kx, there, 128 * half : 128 * half + 128] = tiles[a] if 0 <= a < 4 else blank
            for zi in range(4):
                for pair in range(3):
                    start = (2 - ky) * WINDOW + 128 * pair
                    a = zi - 2 * pair + 1 if pair < 2 else {0: 3, 3: 0}.get(zi, -1)
                    backward[2 - kx, zi * C : zi * C + C, start : start + 128] = (
                        tiles[a] if 0 <= a < 4 else blank
                    )


def planes_of(win, slot, count=1):
    if isinstance(slot, int):
        return win[slot * 256 : (slot + count) * 256, :]
    return win[pl.ds(pl.multiple_of(slot * 256, 256), count * 256), :]


def convolve_own(win, slot, weight, out, product=dot):
    middle = product(planes_of(win, slot, 2), weight[1])
    out[0:256, :] = middle[:256] + product(planes_of(win, slot + 1), weight[2])
    out[256:512, :] = middle[256:] + product(planes_of(win, slot), weight[0])


def add_outer(win, slot, weight, out, side, product=dot):
    at = pl.ds(pl.multiple_of(side * 256, 256), 256)
    out[at, :] += product(planes_of(win, slot), weight[2 * side])


def kernel_gradient(flipped, win, first, product, flat, ready):
    low_half = lax.broadcasted_iota(jnp.int32, (32, 128), 1) < C

    for e in range(3):
        pair = jnp.concatenate([planes_of(flipped, e), planes_of(flipped, e + 1)], axis=1)
        whole = dot(pair, planes_of(win, first, 2))
        for tile in range(9):
            product[tile, e * 256 : e * 256 + 256, :] = whole[:, tile * 128 : tile * 128 + 128]
        for ky in range(3):
            column = (2 - ky) * 3

            def part(zi, tile, parity):
                return product[column + tile, pl.ds(e * 256 + zi * C + parity, 32, stride=2), :]

            sums = {}
            for parity in range(2):
                sums[0, parity] = (
                    part(1, 1, parity) + part(3, 2, parity),
                    part(0, 0, parity) + part(2, 1, parity),
                )
                sums[1, parity] = (
                    part(0, 0, parity) + part(2, 1, parity),
                    part(1, 0, parity) + part(3, 1, parity),
                )
                sums[2, parity] = (
                    part(1, 0, parity) + part(3, 1, parity),
                    part(0, 2, parity) + part(2, 0, parity),
                )
            for kz in range(3):
                low0, high0 = sums[kz, 0]
                low1, high1 = sums[kz, 1]
                straight = jnp.where(low_half, low0, high1)
                crossed = jnp.where(low_half, low1, high0)
                tap = (e * 3 + ky) * 3 + kz
                flat[tap * 32 : tap * 32 + 32, :] = straight + pltpu.roll(crossed, C, 1)
        ready(e)


def kernel(
    vol_hbm,
    cot_hbm,
    w1_hbm,
    w2_hbm,
    feat_hbm,
    back_hbm,
    first_out,
    second_out,
    vol,
    cot,
    w1,
    w2,
    ahead1,
    back1,
    ahead2,
    back2,
    win_v,
    win_h,
    win_g2,
    win_g1,
    flipped_v,
    flipped_h,
    hid,
    g2,
    g1,
    feat,
    back,
    pre,
    own_pre,
    acc,
    product,
    flat,
    near,
    near_in,
    far,
    far_in,
    load_sem,
    store_sem,
    vol_send,
    vol_recv,
    g_send,
    g_recv,
    near_send,
    near_recv,
    far_send,
    far_recv,
    *,
    slabs,
    scale,
):
    sample = lax.axis_index("sample")
    slab = lax.axis_index("slab")
    y, z_hi = sample // 2, sample % 2
    z_lo, x, core = slab // 8, (slab % 8) // 2, slab % 2
    z = z_hi * 4 + z_lo

    def near_partner(r):
        return (lax.rem(y + r // 4, 4) * 2 + z_hi, z_lo * 8 + lax.rem(x + r % 4, 4) * 2 + core)

    def far_partner(r):
        zz = lax.rem(z + r // 2, 8)
        return (y * 2 + lax.div(zz, 4), lax.rem(zz, 4) * 8 + x * 2 + lax.rem(core + r % 2, 2))

    alone = pl.when(slab >= 0)

    has_low = slab > 0
    has_high = slab < slabs - 1
    low = (sample, slab - 1)
    high = (sample, slab + 1)

    barrier = pltpu.get_barrier_semaphore()

    def near_hops(r):
        return min(r // 4, 4 - r // 4) + min(r % 4, 4 - r % 4)

    def far_hops(r):
        return min(r // 2, 8 - r // 2)

    def greet(least, most):
        for hops in range(most, least - 1, -1):
            for r in range(1, 16):
                if near_hops(r) == hops:
                    pl.semaphore_signal(barrier, inc=1, device_id=near_partner(r), device_id_type=MESH)
                if far_hops(r) == hops:
                    pl.semaphore_signal(barrier, inc=1, device_id=far_partner(r), device_id_type=MESH)

    greet(3, 4)

    @pl.when(has_low)
    def _():
        pl.semaphore_signal(barrier, inc=1, device_id=low, device_id_type=MESH)

    @pl.when(has_high)
    def _():
        pl.semaphore_signal(barrier, inc=1, device_id=high, device_id_type=MESH)

    greet(0, 2)

    loads = [
        pltpu.make_async_copy(w1_hbm, w1, load_sem.at[0]),
        pltpu.make_async_copy(vol_hbm.at[0], vol.at[2:4], load_sem.at[1]),
        pltpu.make_async_copy(w2_hbm, w2, load_sem.at[2]),
        pltpu.make_async_copy(cot_hbm.at[0], cot, load_sem.at[3]),
    ]
    for load in loads:
        load.start()

    neighbours = has_low.astype(jnp.int32) + has_high.astype(jnp.int32)
    pl.semaphore_wait(barrier, 30 + neighbours)

    def to_low(plane):
        return pltpu.make_async_remote_copy(
            vol_hbm.at[0, plane], vol.at[4 + plane], vol_send.at[plane], vol_recv.at[2 + plane], low, MESH
        )

    def to_high(plane):
        return pltpu.make_async_remote_copy(
            vol_hbm.at[0, plane], vol.at[plane], vol_send.at[2 + plane], vol_recv.at[plane], high, MESH
        )

    def on_side(side, act_low, act_high):
        pl.when(jnp.logical_and(side == 0, has_low))(act_low)
        pl.when(jnp.logical_and(side == 1, has_high))(act_high)

    def side_of(i):
        return lax.rem(1 - core + i, 2)

    over_link, on_chip = side_of(1), side_of(0)
    on_side(over_link, lambda: to_low(0).start(), lambda: to_high(1).start())
    on_side(on_chip, lambda: to_low(0).start(), lambda: to_high(1).start())
    on_side(over_link, lambda: to_low(1).start(), lambda: to_high(0).start())
    on_side(on_chip, lambda: to_low(1).start(), lambda: to_high(0).start())

    no_plane = jnp.zeros((CELLS, MERGED), BF16)

    @pl.when(jnp.logical_not(has_low))
    def _():
        for buffer, slots in ((vol, (0, 1)), (g2, (0,)), (g1, (0,))):
            for slot in slots:
                buffer[slot] = no_plane

    @pl.when(jnp.logical_not(has_high))
    def _():
        for buffer, slots in ((vol, (4, 5)), (g2, (3,)), (g1, (3,))):
            for slot in slots:
                buffer[slot] = no_plane

    flat[TAPROWS : TAPROWS + 8, :] = jnp.zeros((8, 128), F32)
    def prepare_pair(src, win, slots):
        def body(i, carry):
            slot = slots[0] + i * (slots[1] - slots[0])
            prepare(src, slot, win, slot)
            return carry

        lax.fori_loop(0, 2, body, 0)

    def hide(source, at, plane, keep):
        for j in range(QUADS):
            value = source[pl.ds(pl.multiple_of(at + j * CELLS, CELLS), CELLS), :]
            value = value * sigmoid(value)
            if keep is not None:
                value = jnp.where(keep, value, 0.0)
            hid[plane, :, j * 256 : j * 256 + 256] = value.astype(BF16)

    loads[0].wait()
    expand_weight(w1, ahead1, back1)
    loads[1].wait()
    prepare_pair(vol, win_v, (2, 3))

    def flip_own(i, carry):
        transpose_plane(win_v, 2 + i, flipped_v, 1 + i)
        return carry

    lax.fori_loop(0, 2, flip_own, 0)

    @alone
    def _():
        convolve_own(win_v, 2, ahead1, own_pre)
        pre[0:256, :] = dot(planes_of(win_v, 2), ahead1[2])
        pre[256:512, :] = dot(planes_of(win_v, 3), ahead1[0])

    loads[2].wait()
    expand_weight(w2, ahead2, back2)

    def halo(buffer, which, side):
        if side == 0:
            return pltpu.make_async_remote_copy(
                buffer.at[1], buffer.at[3], g_send.at[2 * which], g_recv.at[2 * which], low, MESH
            )
        return pltpu.make_async_remote_copy(
            buffer.at[2], buffer.at[0], g_send.at[2 * which + 1], g_recv.at[2 * which + 1], high, MESH
        )

    def second_stage(plane, carry):
        for j in range(QUADS):
            value = acc[pl.ds(pl.multiple_of(plane * 256 + j * CELLS, CELLS), CELLS), :]
            gate = sigmoid(value)
            cols = slice(j * 256, j * 256 + 256)
            feat[plane, :, cols] = (value * gate).astype(BF16)
            slope = gate * (1.0 + value * (1.0 - gate))
            g2[plane + 1, :, cols] = (cot[plane, :, cols].astype(F32) * slope).astype(BF16)
        return carry

    def send_side(buffer, which, side):
        on_side(side, lambda: halo(buffer, which, 0).start(), lambda: halo(buffer, which, 1).start())

    loads[3].wait()

    def volume_side(i, carry):
        side = side_of(i)
        on_side(side, lambda: to_high(1).wait_recv(), lambda: to_low(0).wait_recv())
        slot = 1 + 3 * side
        prepare(vol, slot, win_v, slot)

        @alone
        def _():
            add_outer(win_v, slot, ahead1, own_pre, side)
            at = pl.ds(pl.multiple_of(side * 256, 256), 256)
            pre[at, :] += dot(planes_of(win_v, slot), ahead1[1])

        hide(own_pre, side * 256, 1 + side, None)
        prepare(hid, 1 + side, win_h, 1 + side)

        @pl.when(i == 1)
        def _():
            convolve_own(win_h, 1, ahead2, acc)
            add_outer(win_h, 3 * on_chip, ahead2, acc, on_chip)
            second_stage(on_chip, 0)
            send_side(g2, 0, on_chip)

        on_side(side, lambda: to_high(0).wait_recv(), lambda: to_low(1).wait_recv())
        prepare(vol, 5 * side, win_v, 5 * side)

        @alone
        def _():
            add_outer(win_v, 5 * side, ahead1, pre, side)

        inside = jnp.logical_or(jnp.logical_and(side == 0, has_low), jnp.logical_and(side == 1, has_high))
        hide(pre, side * 256, 3 * side, inside)
        prepare(hid, 3 * side, win_h, 3 * side)
        return carry

    lax.fori_loop(0, 2, volume_side, 0)

    @alone
    def _():
        add_outer(win_h, 3 * over_link, ahead2, acc, over_link)

    second_stage(over_link, 0)
    send_side(g2, 0, over_link)
    features_store = pltpu.make_async_copy(feat, feat_hbm.at[0], store_sem.at[0])
    features_store.start()

    me_near = y * 4 + x

    def near_copy(which, r):
        other = lax.rem(y + r // 4, 4) * 4 + lax.rem(x + r % 4, 4)
        return pltpu.make_async_remote_copy(
            near.at[which, other],
            near_in.at[which, r],
            near_send.at[which, r],
            near_recv.at[which, r],
            near_partner(r),
            MESH,
        )

    def far_copy(which, r):
        zz = lax.rem(z + r // 2, 8)
        return pltpu.make_async_remote_copy(
            far.at[which, zz], far_in.at[which, r], far_send.at[which, r], far_recv.at[which, r], far_partner(r), MESH
        )

    def each(copy, what, which):
        for r in range(1, 16):
            getattr(copy(which, r), what)()

    def send_near(which, e):
        for yy in (0,), (1,), (2, 3):
            if yy[0] != e:
                continue
            for to in yy:
                away = lax.rem(to - y + 4, 4)
                for xx in range(4):
                    for pair in range(4):
                        starts = [to * 216 + (2 * pair + i) * 27 + (27 * xx) // 4 for i in range(2)]
                        both = jnp.concatenate([flat[pl.ds(s, 8), :] for s in starts], axis=0)
                        near[which, to * 4 + xx, 16 * pair : 16 * pair + 16, :] = both.astype(BF16)
                for rx in (2, 1, 3, 0):
                    other = lax.rem(x + rx, 4)
                    copy = pltpu.make_async_remote_copy(
                        near.at[which, to * 4 + other],
                        near_in.at[which, away * 4 + rx],
                        near_send.at[which, away * 4 + rx],
                        near_recv.at[which, away * 4 + rx],
                        (to * 2 + z_hi, z_lo * 8 + other * 2 + core),
                        MESH,
                    )
                    if rx:
                        copy.start()
                    else:
                        pl.when(away != 0)(copy.start)

    far_order = sorted(range(1, 16), key=lambda r: -far_hops(r))

    def send_far(which):
        each(near_copy, "wait_recv", which)
        total = near[which, me_near].astype(F32)
        for r in range(1, 16):
            total = total + near_in[which, r].astype(F32)
        for zz in range(8):
            far[which, zz] = total[8 * zz : 8 * zz + 8]
        for r in far_order:
            far_copy(which, r).start()

    lane = lax.broadcasted_iota(jnp.int32, (8, 128), 1)
    begin = (96 * x) % 128 + 432 * core
    skip_rows, skip_lanes = begin // 128, begin % 128

    def finish(which, out):
        for r in reversed(far_order):
            far_copy(which, r).wait_recv()
        total = far[which, z]
        for r in range(1, 16):
            total = total + far_in[which, r]
        total = pltpu.roll(total * scale, (128 - skip_lanes) % 128, 1)
        upper = pltpu.roll(total, (8 - skip_rows) % 8, 0)
        lower = pltpu.roll(total, (8 - skip_rows + 7) % 8, 0)
        out[...] = jnp.where(lane < 128 - skip_lanes, upper, lower)

    prepare_pair(g2, win_g2, (1, 2))

    def flip_planes(win, first, out):
        def body(i, carry):
            transpose_plane(win, first + i, out, i)
            return carry

        lax.fori_loop(0, 4, body, 0)

    flip_planes(win_h, 0, flipped_h)
    kernel_gradient(flipped_h, win_g2, 1, product, flat, functools.partial(send_near, 1))

    def flip_outer(i, carry):
        transpose_plane(win_v, 1 + 3 * i, flipped_v, 3 * i)
        return carry

    lax.fori_loop(0, 2, flip_outer, 0)

    @alone
    def _():
        convolve_own(win_g2, 1, back2, acc, dot_transposed)

    def first_stage(plane, carry):
        for j in range(QUADS):
            at = pl.ds(pl.multiple_of(plane * 256 + j * CELLS, CELLS), CELLS)
            value = own_pre[at, :]
            gate = sigmoid(value)
            slope = gate * (1.0 + value * (1.0 - gate))
            g1[plane + 1, :, j * 256 : j * 256 + 256] = (acc[at, :] * slope).astype(BF16)
        return carry

    def receive_side(buffer, which, side):
        on_side(
            side,
            lambda: halo(buffer, which, 1).wait_recv(),
            lambda: halo(buffer, which, 0).wait_recv(),
        )

    def g2_side(i, carry):
        side = side_of(i)
        receive_side(g2, 0, side)
        prepare(g2, 3 * side, win_g2, 3 * side)

        @alone
        def _():
            add_outer(win_g2, 3 * side, back2, acc, side, dot_transposed)

        first_stage(side, 0)
        send_side(g1, 1, side)
        prepare(g1, 1 + side, win_g1, 1 + side)

        return carry

    lax.fori_loop(0, 2, g2_side, 0)
    kernel_gradient(flipped_v, win_g1, 1, product, flat, functools.partial(send_near, 0))

    @alone
    def _():
        convolve_own(win_g1, 1, back1, acc, dot_transposed)

    send_far(1)

    def g1_side(i, carry):
        side = side_of(i)
        receive_side(g1, 1, side)
        prepare(g1, 3 * side, win_g1, 3 * side)

        @alone
        def _():
            add_outer(win_g1, 3 * side, back1, acc, side, dot_transposed)

        return carry

    lax.fori_loop(0, 2, g1_side, 0)
    for plane in range(2):
        for j in range(QUADS):
            at = (plane * QUADS + j) * CELLS
            back[plane, :, j * 256 : j * 256 + 256] = acc[at : at + CELLS, :].astype(BF16)
    back_store = pltpu.make_async_copy(back, back_hbm.at[0], store_sem.at[1])
    back_store.start()

    send_far(0)
    finish(1, second_out)
    finish(0, first_out)

    @pl.when(has_low)
    def _():
        to_low(0).wait_send()
        to_low(1).wait_send()
        halo(g2, 0, 0).wait_send()
        halo(g1, 1, 0).wait_send()

    @pl.when(has_high)
    def _():
        to_high(0).wait_send()
        to_high(1).wait_send()
        halo(g2, 0, 1).wait_send()
        halo(g1, 1, 1).wait_send()

    for which in range(2):
        each(near_copy, "wait_send", which)
        each(far_copy, "wait_send", which)
    features_store.wait()
    back_store.wait()


def hand_over(feat_in, back_in, first_in, second_in, feat_out, back_out, first_out, second_out):
    feat_out[...] = feat_in[...]
    back_out[...] = back_in[...]
    for source, target in ((first_in, first_out), (second_in, second_out)):
        for row in range(3):
            target[pl.ds(row * 128, 128)] = source[row]
        target[pl.ds(384, 48)] = source[3, :48]


def per_device(volume, cotangent, first_weight, second_weight, *, slabs, voxels):
    vmem = lambda shape, dtype=BF16: pltpu.VMEM(shape, dtype)
    scratch = [
        vmem((6, CELLS, MERGED)),
        vmem((2, CELLS, MERGED)),
        vmem((3, 3, 3, C, C)),
        vmem((3, 3, 3, C, C)),
        vmem((3, WIDE, 256)),
        vmem((3, 256, WIDE)),
        vmem((3, WIDE, 256)),
        vmem((3, 256, WIDE)),
        vmem((6 * 256, WIDE)),
        vmem((4 * 256, WIDE)),
        vmem((4 * 256, WIDE)),
        vmem((4 * 256, WIDE)),
        vmem((1024, 256)),
        vmem((1024, 256)),
        vmem((4, CELLS, MERGED)),
        vmem((4, CELLS, MERGED)),
        vmem((4, CELLS, MERGED)),
        vmem((2, CELLS, MERGED)),
        vmem((2, CELLS, MERGED)),
        vmem((512, 256), F32),
        vmem((512, 256), F32),
        vmem((512, 256), F32),
        vmem((9, 768, 128), F32),
        vmem((TAPROWS + 8, 128), F32),
        vmem((2, 16, 64, 128)),
        vmem((2, 16, 64, 128)),
        vmem((2, 8, 8, 128), F32),
        vmem((2, 16, 8, 128), F32),
        pltpu.SemaphoreType.DMA((4,)),
        pltpu.SemaphoreType.DMA((2,)),
        pltpu.SemaphoreType.DMA((4,)),
        pltpu.SemaphoreType.DMA((4,)),
        pltpu.SemaphoreType.DMA((4,)),
        pltpu.SemaphoreType.DMA((4,)),
        pltpu.SemaphoreType.DMA((2, 16)),
        pltpu.SemaphoreType.DMA((2, 16)),
        pltpu.SemaphoreType.DMA((2, 16)),
        pltpu.SemaphoreType.DMA((2, 16)),
    ]
    anywhere = pl.BlockSpec(memory_space=pl.ANY)
    in_vmem = pl.BlockSpec(memory_space=pltpu.VMEM)
    features, back, first, second = pl.pallas_call(
        functools.partial(kernel, slabs=slabs, scale=1.0 / math.sqrt(voxels)),
        out_shape=(
            jax.ShapeDtypeStruct(volume.shape, BF16),
            jax.ShapeDtypeStruct(volume.shape, BF16),
            jax.ShapeDtypeStruct((8, 128), F32),
            jax.ShapeDtypeStruct((8, 128), F32),
        ),
        in_specs=[anywhere] * 4,
        out_specs=(anywhere, anywhere, in_vmem, in_vmem),
        scratch_shapes=scratch,
        compiler_params=pltpu.CompilerParams(
            collective_id=0, has_side_effects=True, vmem_limit_bytes=63 * 2**20
        ),
    )(volume, cotangent, first_weight, second_weight)
    return pl.pallas_call(
        hand_over,
        out_shape=(
            jax.ShapeDtypeStruct(volume.shape, BF16),
            jax.ShapeDtypeStruct(volume.shape, BF16),
            jax.ShapeDtypeStruct((432,), F32),
            jax.ShapeDtypeStruct((432,), F32),
        ),
        in_specs=[in_vmem] * 4,
        out_specs=(in_vmem,) * 4,
    )(features, back, first, second)


def solution(mesh):
    slabs = mesh.shape["slab"]
    voxels = 524288
    split = P("sample", "slab", None, None)
    return jax.shard_map(
        functools.partial(per_device, slabs=slabs, voxels=voxels),
        mesh=mesh,
        in_specs=(split, split, P(), P()),
        out_specs=(split, split, P(("sample", "slab")), P(("sample", "slab"))),
        check_vma=False,
    )
```

```python
import functools
import math

import jax
import jax.numpy as jnp
from jax import lax
from jax.experimental import pallas as pl
from jax.experimental.pallas import tpu as pltpu
from jax.sharding import PartitionSpec as P

MESH = pl.DeviceIdType.MESH
BF16 = jnp.bfloat16
F32 = jnp.float32

C = 64
CELLS = 32
MERGED = 2048
QUADS = 8
WINDOW = 384
WIDE = 3 * WINDOW
TAPROWS = 864
OFFSETS = (0, 1, 2, 3, 4, -1)


def dot(a, b):
    return lax.dot_general(a, b, (((1,), (0,)), ((), ())), preferred_element_type=F32)


def dot_transposed(a, b):
    return lax.dot_general(a, b, (((1,), (1,)), ((), ())), preferred_element_type=F32)


def sigmoid(v):
    return 0.5 * jnp.tanh(0.5 * v) + 0.5


def prepare(src, plane, win, slot):
    rows = lax.broadcasted_iota(jnp.int32, (CELLS, 128), 0)
    low_half = lax.broadcasted_iota(jnp.int32, (CELLS, 128), 1) < C
    base = slot * 256

    def shifted(tile):
        here = src[plane, :, tile * 128 : tile * 128 + 128].astype(F32)
        before = jnp.where(rows == 0, 0.0, pltpu.roll(here, 1, 0))
        after = jnp.where(rows == CELLS - 1, 0.0, pltpu.roll(here, CELLS - 1, 0))
        return before.astype(BF16), here.astype(BF16), after.astype(BF16)

    nothing = jnp.zeros((CELLS, 128), BF16)
    blank = (nothing, nothing, nothing)
    tiles = {-1: blank, 16: blank}
    for tile in range(16):
        tiles[tile] = shifted(tile)
    for j in range(QUADS):
        at = pl.ds(pl.multiple_of(base + j * CELLS, CELLS), CELLS)
        for d in range(3):
            edge = jnp.where(low_half, tiles[2 * j + 2][d], tiles[2 * j - 1][d])
            win[at, d * WINDOW : d * WINDOW + 128] = tiles[2 * j][d]
            win[at, d * WINDOW + 128 : d * WINDOW + 256] = tiles[2 * j + 1][d]
            win[at, d * WINDOW + 256 : d * WINDOW + 384] = edge


def transpose_plane(win, slot, out, to):
    rows = pl.ds(pl.multiple_of(slot * 256, 256), 256)
    out[pl.ds(pl.multiple_of(to * 256, 256), 256), :] = win[rows, WINDOW : WINDOW + 256].T


def expand_weight(weight, forward, backward):
    zero = jnp.zeros((C, C), BF16)
    blank = jnp.zeros((C, 128), BF16)
    both = lambda a, b: jnp.concatenate([a, b], axis=1)
    for kx in range(3):
        for ky in range(3):
            m = [weight[kx, ky, kz] for kz in range(3)]
            tiles = (both(m[0], zero), both(m[1], m[0]), both(m[2], m[1]), both(zero, m[2]))
            for w, offset in enumerate(OFFSETS):
                there = slice(ky * WINDOW + w * C, ky * WINDOW + w * C + C)
                for half in range(2):
                    a = offset - 2 * half + 1
                    forward[kx, there, 128 * half : 128 * half + 128] = tiles[a] if 0 <= a < 4 else blank
            for zi in range(4):
                for pair in range(3):
                    start = (2 - ky) * WINDOW + 128 * pair
                    a = zi - 2 * pair + 1 if pair < 2 else {0: 3, 3: 0}.get(zi, -1)
                    backward[2 - kx, zi * C : zi * C + C, start : start + 128] = (
                        tiles[a] if 0 <= a < 4 else blank
                    )


def planes_of(win, slot, count=1):
    if isinstance(slot, int):
        return win[slot * 256 : (slot + count) * 256, :]
    return win[pl.ds(pl.multiple_of(slot * 256, 256), count * 256), :]


def convolve_own(win, slot, weight, out, product=dot):
    middle = product(planes_of(win, slot, 2), weight[1])
    out[0:256, :] = middle[:256] + product(planes_of(win, slot + 1), weight[2])
    out[256:512, :] = middle[256:] + product(planes_of(win, slot), weight[0])


def add_outer(win, slot, weight, out, side, product=dot):
    at = pl.ds(pl.multiple_of(side * 256, 256), 256)
    out[at, :] += product(planes_of(win, slot), weight[2 * side])


def kernel_gradient(flipped, win, first, product, flat, ready):
    low_half = lax.broadcasted_iota(jnp.int32, (32, 128), 1) < C

    for e in range(3):
        pair = jnp.concatenate([planes_of(flipped, e), planes_of(flipped, e + 1)], axis=1)
        whole = dot(pair, planes_of(win, first, 2))
        for tile in range(9):
            product[tile, e * 256 : e * 256 + 256, :] = whole[:, tile * 128 : tile * 128 + 128]
        for ky in range(3):
            column = (2 - ky) * 3

            def part(zi, tile, parity):
                return product[column + tile, pl.ds(e * 256 + zi * C + parity, 32, stride=2), :]

            sums = {}
            for parity in range(2):
                sums[0, parity] = (
                    part(1, 1, parity) + part(3, 2, parity),
                    part(0, 0, parity) + part(2, 1, parity),
                )
                sums[1, parity] = (
                    part(0, 0, parity) + part(2, 1, parity),
                    part(1, 0, parity) + part(3, 1, parity),
                )
                sums[2, parity] = (
                    part(1, 0, parity) + part(3, 1, parity),
                    part(0, 2, parity) + part(2, 0, parity),
                )
            for kz in range(3):
                low0, high0 = sums[kz, 0]
                low1, high1 = sums[kz, 1]
                straight = jnp.where(low_half, low0, high1)
                crossed = jnp.where(low_half, low1, high0)
                tap = (e * 3 + ky) * 3 + kz
                flat[tap * 32 : tap * 32 + 32, :] = straight + pltpu.roll(crossed, C, 1)
        ready(e)


def kernel(
    vol_hbm,
    cot_hbm,
    w1_hbm,
    w2_hbm,
    feat_hbm,
    back_hbm,
    first_out,
    second_out,
    vol,
    cot,
    w1,
    w2,
    ahead1,
    back1,
    ahead2,
    back2,
    win_v,
    win_h,
    win_g2,
    win_g1,
    flipped_v,
    flipped_h,
    hid,
    g2,
    g1,
    feat,
    back,
    pre,
    own_pre,
    acc,
    product,
    flat,
    near,
    near_in,
    far,
    far_in,
    load_sem,
    store_sem,
    vol_send,
    vol_recv,
    g_send,
    g_recv,
    near_send,
    near_recv,
    far_send,
    far_recv,
    *,
    slabs,
    scale,
):
    sample = lax.axis_index("sample")
    slab = lax.axis_index("slab")
    y, z_hi = sample // 2, sample % 2
    z_lo, x, core = slab // 8, (slab % 8) // 2, slab % 2
    z = z_hi * 4 + z_lo

    def near_partner(r):
        return (lax.rem(y + r // 4, 4) * 2 + z_hi, z_lo * 8 + lax.rem(x + r % 4, 4) * 2 + core)

    def far_partner(r):
        zz = lax.rem(z + r // 2, 8)
        return (y * 2 + lax.div(zz, 4), lax.rem(zz, 4) * 8 + x * 2 + lax.rem(core + r % 2, 2))

    alone = pl.when(slab >= 0)

    has_low = slab > 0
    has_high = slab < slabs - 1
    low = (sample, slab - 1)
    high = (sample, slab + 1)

    barrier = pltpu.get_barrier_semaphore()

    def near_hops(r):
        return min(r // 4, 4 - r // 4) + min(r % 4, 4 - r % 4)

    def far_hops(r):
        return min(r // 2, 8 - r // 2)

    def greet(least, most):
        for hops in range(most, least - 1, -1):
            for r in range(1, 16):
                if near_hops(r) == hops:
                    pl.semaphore_signal(barrier, inc=1, device_id=near_partner(r), device_id_type=MESH)
                if far_hops(r) == hops:
                    pl.semaphore_signal(barrier, inc=1, device_id=far_partner(r), device_id_type=MESH)

    greet(3, 4)

    @pl.when(has_low)
    def _():
        pl.semaphore_signal(barrier, inc=1, device_id=low, device_id_type=MESH)

    @pl.when(has_high)
    def _():
        pl.semaphore_signal(barrier, inc=1, device_id=high, device_id_type=MESH)

    greet(0, 2)

    loads = [
        pltpu.make_async_copy(w1_hbm, w1, load_sem.at[0]),
        pltpu.make_async_copy(vol_hbm.at[0], vol.at[2:4], load_sem.at[1]),
        pltpu.make_async_copy(w2_hbm, w2, load_sem.at[2]),
        pltpu.make_async_copy(cot_hbm.at[0], cot, load_sem.at[3]),
    ]
    for load in loads:
        load.start()

    neighbours = has_low.astype(jnp.int32) + has_high.astype(jnp.int32)
    pl.semaphore_wait(barrier, 30 + neighbours)

    def to_low(plane):
        return pltpu.make_async_remote_copy(
            vol_hbm.at[0, plane], vol.at[4 + plane], vol_send.at[plane], vol_recv.at[2 + plane], low, MESH
        )

    def to_high(plane):
        return pltpu.make_async_remote_copy(
            vol_hbm.at[0, plane], vol.at[plane], vol_send.at[2 + plane], vol_recv.at[plane], high, MESH
        )

    def on_side(side, act_low, act_high):
        pl.when(jnp.logical_and(side == 0, has_low))(act_low)
        pl.when(jnp.logical_and(side == 1, has_high))(act_high)

    def side_of(i):
        return lax.rem(1 - core + i, 2)

    over_link, on_chip = side_of(1), side_of(0)
    on_side(over_link, lambda: to_low(0).start(), lambda: to_high(1).start())
    on_side(on_chip, lambda: to_low(0).start(), lambda: to_high(1).start())
    on_side(over_link, lambda: to_low(1).start(), lambda: to_high(0).start())
    on_side(on_chip, lambda: to_low(1).start(), lambda: to_high(0).start())

    no_plane = jnp.zeros((CELLS, MERGED), BF16)

    @pl.when(jnp.logical_not(has_low))
    def _():
        for buffer, slots in ((vol, (0, 1)), (g2, (0,)), (g1, (0,))):
            for slot in slots:
                buffer[slot] = no_plane

    @pl.when(jnp.logical_not(has_high))
    def _():
        for buffer, slots in ((vol, (4, 5)), (g2, (3,)), (g1, (3,))):
            for slot in slots:
                buffer[slot] = no_plane

    flat[TAPROWS : TAPROWS + 8, :] = jnp.zeros((8, 128), F32)
    def prepare_pair(src, win, slots):
        def body(i, carry):
            slot = slots[0] + i * (slots[1] - slots[0])
            prepare(src, slot, win, slot)
            return carry

        lax.fori_loop(0, 2, body, 0)

    def hide(source, at, plane, keep):
        for j in range(QUADS):
            value = source[pl.ds(pl.multiple_of(at + j * CELLS, CELLS), CELLS), :]
            value = value * sigmoid(value)
            if keep is not None:
                value = jnp.where(keep, value, 0.0)
            hid[plane, :, j * 256 : j * 256 + 256] = value.astype(BF16)

    loads[0].wait()
    expand_weight(w1, ahead1, back1)
    loads[1].wait()
    prepare_pair(vol, win_v, (2, 3))

    def flip_own(i, carry):
        transpose_plane(win_v, 2 + i, flipped_v, 1 + i)
        return carry

    lax.fori_loop(0, 2, flip_own, 0)

    @alone
    def _():
        convolve_own(win_v, 2, ahead1, own_pre)
        pre[0:256, :] = dot(planes_of(win_v, 2), ahead1[2])
        pre[256:512, :] = dot(planes_of(win_v, 3), ahead1[0])

    loads[2].wait()
    expand_weight(w2, ahead2, back2)

    def halo(buffer, which, side):
        if side == 0:
            return pltpu.make_async_remote_copy(
                buffer.at[1], buffer.at[3], g_send.at[2 * which], g_recv.at[2 * which], low, MESH
            )
        return pltpu.make_async_remote_copy(
            buffer.at[2], buffer.at[0], g_send.at[2 * which + 1], g_recv.at[2 * which + 1], high, MESH
        )

    def second_stage(plane, carry):
        for j in range(QUADS):
            value = acc[pl.ds(pl.multiple_of(plane * 256 + j * CELLS, CELLS), CELLS), :]
            gate = sigmoid(value)
            cols = slice(j * 256, j * 256 + 256)
            feat[plane, :, cols] = (value * gate).astype(BF16)
            slope = gate * (1.0 + value * (1.0 - gate))
            g2[plane + 1, :, cols] = (cot[plane, :, cols].astype(F32) * slope).astype(BF16)
        return carry

    def send_side(buffer, which, side):
        on_side(side, lambda: halo(buffer, which, 0).start(), lambda: halo(buffer, which, 1).start())

    loads[3].wait()

    def flip_side(side):
        transpose_plane(win_v, 1 + 3 * side, flipped_v, 3 * side)
        transpose_plane(win_h, 1 + side, flipped_h, 1 + side)
        transpose_plane(win_h, 3 * side, flipped_h, 3 * side)

    def volume_side(i, carry):
        side = side_of(i)
        on_side(side, lambda: to_high(1).wait_recv(), lambda: to_low(0).wait_recv())
        slot = 1 + 3 * side
        prepare(vol, slot, win_v, slot)

        @alone
        def _():
            add_outer(win_v, slot, ahead1, own_pre, side)
            at = pl.ds(pl.multiple_of(side * 256, 256), 256)
            pre[at, :] += dot(planes_of(win_v, slot), ahead1[1])

        hide(own_pre, side * 256, 1 + side, None)
        prepare(hid, 1 + side, win_h, 1 + side)

        @pl.when(i == 1)
        def _():
            convolve_own(win_h, 1, ahead2, acc)
            add_outer(win_h, 3 * on_chip, ahead2, acc, on_chip)
            second_stage(on_chip, 0)
            send_side(g2, 0, on_chip)

        on_side(side, lambda: to_high(0).wait_recv(), lambda: to_low(1).wait_recv())
        prepare(vol, 5 * side, win_v, 5 * side)

        @alone
        def _():
            add_outer(win_v, 5 * side, ahead1, pre, side)

        inside = jnp.logical_or(jnp.logical_and(side == 0, has_low), jnp.logical_and(side == 1, has_high))
        hide(pre, side * 256, 3 * side, inside)
        prepare(hid, 3 * side, win_h, 3 * side)

        @pl.when(i == 0)
        def _():
            flip_side(side)

        return carry

    lax.fori_loop(0, 2, volume_side, 0)

    @alone
    def _():
        add_outer(win_h, 3 * over_link, ahead2, acc, over_link)

    second_stage(over_link, 0)
    send_side(g2, 0, over_link)
    features_store = pltpu.make_async_copy(feat, feat_hbm.at[0], store_sem.at[0])
    features_store.start()

    me_near = y * 4 + x

    def near_copy(which, r):
        other = lax.rem(y + r // 4, 4) * 4 + lax.rem(x + r % 4, 4)
        return pltpu.make_async_remote_copy(
            near.at[which, other],
            near_in.at[which, r],
            near_send.at[which, r],
            near_recv.at[which, r],
            near_partner(r),
            MESH,
        )

    def far_copy(which, r):
        zz = lax.rem(z + r // 2, 8)
        return pltpu.make_async_remote_copy(
            far.at[which, zz], far_in.at[which, r], far_send.at[which, r], far_recv.at[which, r], far_partner(r), MESH
        )

    def each(copy, what, which):
        for r in range(1, 16):
            getattr(copy(which, r), what)()

    def send_near(which, e):
        for yy in (0,), (1,), (2, 3):
            if yy[0] != e:
                continue
            for to in yy:
                away = lax.rem(to - y + 4, 4)
                for xx in range(4):
                    for pair in range(4):
                        starts = [to * 216 + (2 * pair + i) * 27 + (27 * xx) // 4 for i in range(2)]
                        both = jnp.concatenate([flat[pl.ds(s, 8), :] for s in starts], axis=0)
                        near[which, to * 4 + xx, 16 * pair : 16 * pair + 16, :] = both.astype(BF16)
                for rx in (2, 1, 3, 0):
                    other = lax.rem(x + rx, 4)
                    copy = pltpu.make_async_remote_copy(
                        near.at[which, to * 4 + other],
                        near_in.at[which, away * 4 + rx],
                        near_send.at[which, away * 4 + rx],
                        near_recv.at[which, away * 4 + rx],
                        (to * 2 + z_hi, z_lo * 8 + other * 2 + core),
                        MESH,
                    )
                    if rx:
                        copy.start()
                    else:
                        pl.when(away != 0)(copy.start)

    far_order = sorted(range(1, 16), key=lambda r: -far_hops(r))

    def send_far(which):
        each(near_copy, "wait_recv", which)
        total = near[which, me_near].astype(F32)
        for r in range(1, 16):
            total = total + near_in[which, r].astype(F32)
        for zz in range(8):
            far[which, zz] = total[8 * zz : 8 * zz + 8]
        for r in far_order:
            far_copy(which, r).start()

    lane = lax.broadcasted_iota(jnp.int32, (8, 128), 1)
    begin = (96 * x) % 128 + 432 * core
    skip_rows, skip_lanes = begin // 128, begin % 128

    def finish(which, out):
        for r in reversed(far_order):
            far_copy(which, r).wait_recv()
        total = far[which, z]
        for r in range(1, 16):
            total = total + far_in[which, r]
        total = pltpu.roll(total * scale, (128 - skip_lanes) % 128, 1)
        upper = pltpu.roll(total, (8 - skip_rows) % 8, 0)
        lower = pltpu.roll(total, (8 - skip_rows + 7) % 8, 0)
        out[...] = jnp.where(lane < 128 - skip_lanes, upper, lower)

    prepare_pair(g2, win_g2, (1, 2))

    flip_side(over_link)
    kernel_gradient(flipped_h, win_g2, 1, product, flat, functools.partial(send_near, 1))

    @alone
    def _():
        convolve_own(win_g2, 1, back2, acc, dot_transposed)

    def first_stage(plane, carry):
        for j in range(QUADS):
            at = pl.ds(pl.multiple_of(plane * 256 + j * CELLS, CELLS), CELLS)
            value = own_pre[at, :]
            gate = sigmoid(value)
            slope = gate * (1.0 + value * (1.0 - gate))
            g1[plane + 1, :, j * 256 : j * 256 + 256] = (acc[at, :] * slope).astype(BF16)
        return carry

    def receive_side(buffer, which, side):
        on_side(
            side,
            lambda: halo(buffer, which, 1).wait_recv(),
            lambda: halo(buffer, which, 0).wait_recv(),
        )

    def g2_side(i, carry):
        side = side_of(i)
        receive_side(g2, 0, side)
        prepare(g2, 3 * side, win_g2, 3 * side)

        @alone
        def _():
            add_outer(win_g2, 3 * side, back2, acc, side, dot_transposed)

        first_stage(side, 0)
        send_side(g1, 1, side)
        prepare(g1, 1 + side, win_g1, 1 + side)

        return carry

    lax.fori_loop(0, 2, g2_side, 0)
    kernel_gradient(flipped_v, win_g1, 1, product, flat, functools.partial(send_near, 0))

    @alone
    def _():
        convolve_own(win_g1, 1, back1, acc, dot_transposed)

    send_far(1)

    def g1_side(i, carry):
        side = side_of(i)
        receive_side(g1, 1, side)
        prepare(g1, 3 * side, win_g1, 3 * side)

        @alone
        def _():
            add_outer(win_g1, 3 * side, back1, acc, side, dot_transposed)

        return carry

    lax.fori_loop(0, 2, g1_side, 0)
    for plane in range(2):
        for j in range(QUADS):
            at = (plane * QUADS + j) * CELLS
            back[plane, :, j * 256 : j * 256 + 256] = acc[at : at + CELLS, :].astype(BF16)
    back_store = pltpu.make_async_copy(back, back_hbm.at[0], store_sem.at[1])
    back_store.start()

    send_far(0)
    finish(1, second_out)
    finish(0, first_out)

    @pl.when(has_low)
    def _():
        to_low(0).wait_send()
        to_low(1).wait_send()
        halo(g2, 0, 0).wait_send()
        halo(g1, 1, 0).wait_send()

    @pl.when(has_high)
    def _():
        to_high(0).wait_send()
        to_high(1).wait_send()
        halo(g2, 0, 1).wait_send()
        halo(g1, 1, 1).wait_send()

    for which in range(2):
        each(near_copy, "wait_send", which)
        each(far_copy, "wait_send", which)
    features_store.wait()
    back_store.wait()


def hand_over(feat_in, back_in, first_in, second_in, feat_out, back_out, first_out, second_out):
    feat_out[...] = feat_in[...]
    back_out[...] = back_in[...]
    for source, target in ((first_in, first_out), (second_in, second_out)):
        for row in range(3):
            target[pl.ds(row * 128, 128)] = source[row]
        target[pl.ds(384, 48)] = source[3, :48]


def per_device(volume, cotangent, first_weight, second_weight, *, slabs, voxels):
    vmem = lambda shape, dtype=BF16: pltpu.VMEM(shape, dtype)
    scratch = [
        vmem((6, CELLS, MERGED)),
        vmem((2, CELLS, MERGED)),
        vmem((3, 3, 3, C, C)),
        vmem((3, 3, 3, C, C)),
        vmem((3, WIDE, 256)),
        vmem((3, 256, WIDE)),
        vmem((3, WIDE, 256)),
        vmem((3, 256, WIDE)),
        vmem((6 * 256, WIDE)),
        vmem((4 * 256, WIDE)),
        vmem((4 * 256, WIDE)),
        vmem((4 * 256, WIDE)),
        vmem((1024, 256)),
        vmem((1024, 256)),
        vmem((4, CELLS, MERGED)),
        vmem((4, CELLS, MERGED)),
        vmem((4, CELLS, MERGED)),
        vmem((2, CELLS, MERGED)),
        vmem((2, CELLS, MERGED)),
        vmem((512, 256), F32),
        vmem((512, 256), F32),
        vmem((512, 256), F32),
        vmem((9, 768, 128), F32),
        vmem((TAPROWS + 8, 128), F32),
        vmem((2, 16, 64, 128)),
        vmem((2, 16, 64, 128)),
        vmem((2, 8, 8, 128), F32),
        vmem((2, 16, 8, 128), F32),
        pltpu.SemaphoreType.DMA((4,)),
        pltpu.SemaphoreType.DMA((2,)),
        pltpu.SemaphoreType.DMA((4,)),
        pltpu.SemaphoreType.DMA((4,)),
        pltpu.SemaphoreType.DMA((4,)),
        pltpu.SemaphoreType.DMA((4,)),
        pltpu.SemaphoreType.DMA((2, 16)),
        pltpu.SemaphoreType.DMA((2, 16)),
        pltpu.SemaphoreType.DMA((2, 16)),
        pltpu.SemaphoreType.DMA((2, 16)),
    ]
    anywhere = pl.BlockSpec(memory_space=pl.ANY)
    in_vmem = pl.BlockSpec(memory_space=pltpu.VMEM)
    features, back, first, second = pl.pallas_call(
        functools.partial(kernel, slabs=slabs, scale=1.0 / math.sqrt(voxels)),
        out_shape=(
            jax.ShapeDtypeStruct(volume.shape, BF16),
            jax.ShapeDtypeStruct(volume.shape, BF16),
            jax.ShapeDtypeStruct((8, 128), F32),
            jax.ShapeDtypeStruct((8, 128), F32),
        ),
        in_specs=[anywhere] * 4,
        out_specs=(anywhere, anywhere, in_vmem, in_vmem),
        scratch_shapes=scratch,
        compiler_params=pltpu.CompilerParams(
            collective_id=0, has_side_effects=True, vmem_limit_bytes=63 * 2**20
        ),
    )(volume, cotangent, first_weight, second_weight)
    return pl.pallas_call(
        hand_over,
        out_shape=(
            jax.ShapeDtypeStruct(volume.shape, BF16),
            jax.ShapeDtypeStruct(volume.shape, BF16),
            jax.ShapeDtypeStruct((432,), F32),
            jax.ShapeDtypeStruct((432,), F32),
        ),
        in_specs=[in_vmem] * 4,
        out_specs=(in_vmem,) * 4,
    )(features, back, first, second)


def solution(mesh):
    slabs = mesh.shape["slab"]
    voxels = 524288
    split = P("sample", "slab", None, None)
    return jax.shard_map(
        functools.partial(per_device, slabs=slabs, voxels=voxels),
        mesh=mesh,
        in_specs=(split, split, P(), P()),
        out_specs=(split, split, P(("sample", "slab")), P(("sample", "slab"))),
        check_vma=False,
    )
```
